32 devices in a mesh: groups: 2 (over y), expert: 8 (over z, x), replica: 2 (over core).
Axes of the slice: x: 2, y: 2, z: 4, core: 2. Of those that a mesh axis runs over, the one named last changes fastest.
Arguments:
- encoded: bfloat16 [32768, 128], P(('groups', 'expert', 'replica')), parts along dimension 0, may hold values from -6 to 6
- region_id: int32 [32768], P(('groups', 'expert', 'replica')), parts along dimension 0, may hold values from 0 to 15, as said below
- spacing: float32 [32768], P(('groups', 'expert', 'replica')), parts along dimension 0, may hold values from 0.01 to 0.1
- frame_index: int32 [512], P(('groups', 'expert', 'replica')), parts along dimension 0, may hold values from 0 to 255
- target_rgb: float32 [3, 512], P(None, ('groups', 'expert', 'replica')), parts along dimension 1, may hold values from 0 to 1
- frame_code: float32 [3, 512], P(None, 'groups'), parts along dimension 1, may hold values from -4 to 4
- first_weight: bfloat16 [16, 128, 256], P('expert'), may hold values from -0.5 to 0.5
- hidden_weight: bfloat16 [16, 3, 256, 256], P('expert'), may hold values from -0.375 to 0.375
- head_weight: bfloat16 [4, 256], replicated, may hold values from -0.375 to 0.375
Outputs:
- first_grad: float32 [32, 128, 256], P(('groups', 'expert'), 'replica'), parts along dimension 0
- hidden_grad: float32 [32, 3, 256, 256], P(('groups', 'expert'), None, 'replica'), parts along dimension 0
- head_grad: float32 [8, 256], P('groups'), parts along dimension 0
- rendered: float32 [3, 512], P(None, ('groups', 'expert', 'replica')), parts along dimension 1
The draws below stay inside these ranges and needn't reach their ends.
There are 2 independent parts, one for each index of `groups`. The reference program is written for one: setup_inputs(seed, part) draws one part's arguments, and reference() takes and returns one part's arrays. A program takes and returns all parts, laid end to end along the dimension named above; an argument that names none is the same for every part. Nothing has to cross between parts.
Inputs may be any that keep to these rules, and one draw needn't show every extreme that they name: `region_id`: among the samples of one device no region is named more than 128 times, and some region is named exactly 128 times.
All inputs are finite; a program needn't handle non-finite values.
Results may differ from the reference program's by a relative error of at most 0.012.
Values may be sent and summed in bfloat16 or wider, within the bound.
No kernel may reach another device: no remote copies, remote signals or barrier semaphores. Data moves between devices by JAX's collectives and lax.ppermute only.
A program may use at most 64 MiB of HBM per device.

```python
import math
import jax
import jax.numpy as jnp
from jax import lax

ENC = 128
HID = 256
LAYERS = 4
RAY_SAMPLES = 64
FRAMES = 256
SAMP_DEV = 1024
EXPERTS = 16
MOST = 128
SAMPLES = 16384
RAYS = 256


def draw_region_id(key, part):
    blocks = SAMPLES // SAMP_DEV
    hot_expert = jax.random.randint(jax.random.fold_in(key, 7), (), 0, EXPERTS).astype(jnp.int32)
    warm_count = MOST // 2

    def one_block(block_number):
        block_key = jax.random.fold_in(key, block_number + 11)
        others = (hot_expert + 1 + jax.random.permutation(jax.random.fold_in(block_key, 1), EXPERTS - 1).astype(jnp.int32)) % EXPERTS
        position = jnp.arange(SAMP_DEV, dtype=jnp.int32)
        rest_pick = others[1 + (position - MOST - warm_count) % (EXPERTS - 2)]
        values = jnp.where(position < MOST, hot_expert, jnp.where(position < MOST + warm_count, others[0], rest_pick))
        shuffle = jax.random.permutation(jax.random.fold_in(block_key, 2), SAMP_DEV)
        return values[shuffle].astype(jnp.int32)
    return jax.vmap(one_block)(jnp.arange(blocks, dtype=jnp.int32)).reshape(-1).astype(jnp.int32)


def plant(drawn, stream_key, low, top_value):
    longest = drawn.shape.index(max(drawn.shape))
    spots = []
    for shift in (0, 1):
        where = [jax.random.randint(jax.random.fold_in(stream_key, axis), (), 0, length) for axis, length in enumerate(drawn.shape)]
        where[longest] = (where[longest] + shift) % drawn.shape[longest]
        spots.append(tuple(where))
    return drawn.at[spots[0]].set(low).at[spots[1]].set(top_value)


def block_scale(rng, shape, pieces, low, high):
    gain = 1.0
    for axis_at, blocks in pieces:
        heights = jax.random.uniform(jax.random.fold_in(jax.random.fold_in(rng, 6), axis_at), (blocks,), jnp.float32, low / len(pieces), high / len(pieces))
        gain = gain * jnp.repeat(jnp.exp(heights), shape[axis_at] // blocks).reshape((-1,) + (1,) * (len(shape) - 1 - axis_at))
    return gain


def centred(rng, shape, width, most, pieces=(), kind=jnp.bfloat16):
    gain = block_scale(rng, shape, pieces, -0.22, 0.18) if pieces else 1.0
    drawn = jax.random.normal(rng, shape, jnp.float32) * width * gain
    return jnp.minimum(jnp.maximum(drawn, -most), most).astype(kind)


def setup_inputs(seed: int = 0, part: int = 0) -> dict:
    seeds = jax.random.split(jax.random.key(seed), 10)
    own_keys = jax.random.split(jax.random.fold_in(seeds[9], part), 10)
    encoded = centred(own_keys[0], (SAMPLES, ENC), 1.0, 6.0, ((0, 16),))
    region_id = draw_region_id(jax.random.fold_in(jax.random.fold_in(seeds[9], part), 71), part)
    spacing = jnp.clip(jnp.exp(math.log(0.1) - 2.3025851 * jax.random.uniform(own_keys[2], (SAMPLES,), jnp.float32) ** block_scale(own_keys[2], (SAMPLES,), ((0, 16),), -0.2, 0.2)), 0.01, 0.1)
    frame_index = plant(jax.random.randint(own_keys[3], (RAYS,), 0, FRAMES), jax.random.fold_in(own_keys[3], 1), 0, FRAMES - 1).astype(jnp.int32)
    target_rgb = jnp.clip(1.0 * jax.random.uniform(own_keys[4], (3, RAYS), jnp.float32) ** block_scale(own_keys[4], (3, RAYS), ((1, 16),), -0.2, 0.2), 0.0, 1.0)
    frame_code = centred(own_keys[5], (3, FRAMES), 1.0, 4.0, (), jnp.float32)
    first_weight = centred(seeds[6], (EXPERTS, ENC, HID), ENC ** -0.5, 0.5, ((0, 8),))
    hidden_weight = centred(seeds[7], (EXPERTS, LAYERS - 1, HID, HID), HID ** -0.5, 0.375, ((0, 8),))
    head_weight = centred(seeds[8], (4, HID), HID ** -0.5, 0.375)
    return dict(encoded=encoded, region_id=region_id, spacing=spacing, frame_index=frame_index, target_rgb=target_rgb, frame_code=frame_code, first_weight=first_weight, hidden_weight=hidden_weight, head_weight=head_weight)


def silu_slope(linear):
    sigmoid_val = jax.nn.sigmoid(linear)
    return sigmoid_val * (1.0 + linear * (1.0 - sigmoid_val))

def composite(raw_in, spacing, frame_bias, target_rgb):
    ray_count = spacing.shape[0] // RAY_SAMPLES
    density = jax.nn.softplus(raw_in[0]).reshape(ray_count, RAY_SAMPLES)
    optical = density * spacing.reshape(ray_count, RAY_SAMPLES)
    before = jnp.cumsum(optical, axis=1) - optical
    weight = jnp.exp(-before) * (1.0 - jnp.exp(-optical))
    colour = jax.nn.sigmoid(raw_in[1:].reshape(3, ray_count, RAY_SAMPLES) + frame_bias[:, :, None])
    rendered = lax.optimization_barrier(jnp.sum(weight[None] * colour, axis=2)) + (1.0 - lax.optimization_barrier(jnp.sum(weight, axis=1)))[None]
    loss_value = 0.5 * jnp.sum((rendered - target_rgb) ** 2)
    return (loss_value, rendered)

def block_slots(region_block):
    onehot = (region_block[:, None] == jnp.arange(EXPERTS, dtype=jnp.int32)[None, :]).astype(jnp.int32)
    running = jnp.cumsum(onehot, axis=0).astype(jnp.int32)
    return (lax.optimization_barrier(jnp.sum(running * onehot, axis=1)) - 1).astype(jnp.int32)

def layer_pass(row_block, first_w, hidden_w):
    activations = [row_block]
    slopes = []
    current = row_block
    for layer_index in range(LAYERS):
        weight = first_w if layer_index == 0 else hidden_w[layer_index - 1]
        linear = jnp.dot(current, weight, preferred_element_type=jnp.float32)
        slopes.append(lax.optimization_barrier(silu_slope(linear).astype(jnp.bfloat16)))
        current = lax.optimization_barrier(jax.nn.silu(linear).astype(jnp.bfloat16))
        activations.append(current)
    return (activations, slopes)

def reference(encoded, region_id, spacing, frame_index, target_rgb, frame_code, first_weight, hidden_weight, head_weight):
    blocks = SAMPLES // SAMP_DEV
    capacity = blocks * MOST
    slots = jax.vmap(block_slots)(region_id.reshape(blocks, SAMP_DEV)).reshape(-1)
    block_of = (jnp.arange(SAMPLES, dtype=jnp.int32) // SAMP_DEV).astype(jnp.int32)
    slot_index = (region_id * capacity + block_of * MOST + slots).astype(jnp.int32)
    buffer = jnp.zeros((EXPERTS * capacity, ENC), jnp.bfloat16).at[slot_index].set(encoded)
    buffer = buffer.reshape(EXPERTS, capacity, ENC)

    def head_of(expert_item):
        row_block, first_w, hidden_w = expert_item
        activations, slopes = layer_pass(row_block, first_w, hidden_w)
        return jnp.dot(activations[-1], head_weight.T, preferred_element_type=jnp.float32)
    raw_out = lax.map(head_of, (buffer, first_weight, hidden_weight))
    raw_t = raw_out.reshape(EXPERTS * capacity, 4)[slot_index].T
    frame_hot = (frame_index[None, :] == jnp.arange(FRAMES, dtype=jnp.int32)[:, None]).astype(jnp.float32)
    frame_bias = jnp.dot(frame_code, frame_hot, precision=lax.Precision.HIGHEST)
    loss_value, pullback, rendered = jax.vjp(lambda raw_in: composite(raw_in, spacing, frame_bias, target_rgb), raw_t, has_aux=True)
    graw_t = pullback(jnp.ones((), jnp.float32))[0]
    graw_back = jnp.zeros((EXPERTS * capacity, 4), jnp.float32).at[slot_index].set(graw_t.T)
    graw_back = graw_back.reshape(EXPERTS, capacity, 4)
    head_w32 = head_weight.astype(jnp.float32)

    def grads_of(expert_item):
        row_block, first_w, hidden_w, graw_rows = expert_item
        activations, slopes = layer_pass(row_block, first_w, hidden_w)
        head_part = jnp.dot(graw_rows.T, activations[-1].astype(jnp.float32), precision=lax.Precision.HIGHEST)
        upstream = lax.optimization_barrier(jnp.dot(graw_rows, head_w32, precision=lax.Precision.HIGHEST).astype(jnp.bfloat16))
        grads = [None] * LAYERS
        for layer_index in reversed(range(LAYERS)):
            weight = first_w if layer_index == 0 else hidden_w[layer_index - 1]
            grad_linear = (upstream.astype(jnp.float32) * slopes[layer_index].astype(jnp.float32)).astype(jnp.bfloat16)
            grads[layer_index] = jnp.dot(activations[layer_index].T, grad_linear, preferred_element_type=jnp.float32)
            if layer_index > 0:
                upstream = lax.optimization_barrier(jnp.dot(grad_linear, weight.T, preferred_element_type=jnp.float32).astype(jnp.bfloat16))
        return (grads[0], jnp.stack(grads[1:], axis=0), head_part)
    first_grad, hidden_grad, head_parts = lax.map(grads_of, (buffer, first_weight, hidden_weight, graw_back))
    return (first_grad, hidden_grad, lax.optimization_barrier(jnp.sum(head_parts, axis=0)), rendered)
```

```python
import functools

import jax
import jax.numpy as jnp
from jax import lax
from jax.experimental import pallas as pl
from jax.experimental.pallas import tpu as pltpu
from jax.sharding import PartitionSpec as P

RAY_SAMPLES = 64
LANES = 128
META = 32
F32 = jnp.float32
BF16 = jnp.bfloat16
VMEM = pltpu.VMEM


def iota(shape, dim):
    return lax.broadcasted_iota(jnp.int32, shape, dim)


def hot(mask, dtype=BF16):
    return jnp.where(mask, 1.0, 0.0).astype(dtype)


def dot(a, b):
    return jnp.dot(a, b, preferred_element_type=F32)


def dot_nt(a, b):
    return lax.dot_general(a, b, (((1,), (1,)), ((), ())), preferred_element_type=F32)


def dot_tn(a, b):
    return lax.dot_general(a, b, (((0,), (0,)), ((), ())), preferred_element_type=F32)


def split(x):
    high = x.astype(BF16)
    return high, (x - high.astype(F32)).astype(BF16)


def lane_row(x):
    return jnp.concatenate([x[k : k + 1] for k in range(x.shape[0])], axis=1)


def ranks(region, experts):
    rows = region.shape[0]
    names = iota((experts, LANES), 0)
    upper = hot(iota((LANES, LANES), 0) <= iota((LANES, LANES), 1))
    equal = [hot(region[k : k + 1] == names, F32) for k in range(rows)]
    running = dot(jnp.concatenate(equal, axis=0).astype(BF16), upper)
    before = jnp.zeros((experts, 1), F32)
    out = []
    for k in range(rows):
        here = running[k * experts : (k + 1) * experts]
        out.append(jnp.sum(equal[k] * (here + before), axis=0, keepdims=True))
        before = before + here[:, LANES - 1 :]
    return jnp.concatenate(out, axis=0).astype(jnp.int32) - 1


def dispatch_kernel(experts, capacity, region_ref, enc_ref, spacing_ref, frame_ref, target_ref, code_ref, out_ref):
    owners, rows = out_ref.shape[0], out_ref.shape[1] - META
    samples = enc_ref.shape[0]
    region = region_ref[...]
    slot = lane_row(region * capacity + ranks(region, experts))
    enc = enc_ref[...]

    chunks = region.shape[0]
    frames = code_ref.shape[1]
    rays = frame_ref.shape[1]
    chosen = hot(frame_ref[...] == iota((frames, rays), 0), F32)
    bias = lax.dot_general(
        code_ref[...], chosen, (((1,), (0,)), ((), ())), precision=lax.Precision.HIGHEST, preferred_element_type=F32
    )
    small = jnp.concatenate([bias, target_ref[...], jnp.zeros((2, rays), F32)], axis=0)
    small_high, small_low = split(small)
    small = jnp.concatenate(
        [small_high.astype(F32), small_low.astype(F32), jnp.zeros((8, LANES - 2 * rays), F32)], axis=1
    )
    spacing_high, spacing_low = split(spacing_ref[...])
    meta = jnp.concatenate(
        [region.astype(F32), spacing_high.astype(F32), spacing_low.astype(F32), small], axis=0
    ).astype(BF16)

    def one(d, carry):
        pick = hot(iota((rows, samples), 0) == slot - d * rows)
        out_ref[d, :rows, :] = dot(pick, enc).astype(BF16)
        out_ref[d, rows:, :] = meta
        return carry

    lax.fori_loop(0, owners, one, 0, unroll=2)


def layer_forward(linear):
    half = jnp.tanh(0.5 * linear)
    gate = 0.5 + 0.5 * half
    act = linear * gate
    slope = gate + act * (1.0 - gate)
    return act.astype(BF16), slope.astype(BF16)


def forward_kernel(capacity, tile, recv_ref, first_ref, hidden_ref, head_ref, act_ref, slope_ref, raw_ref, held):
    sources = recv_ref.shape[0]
    local = first_ref.shape[0]
    layers = hidden_ref.shape[1] + 1
    head = head_ref[...]
    pairs = local * head.shape[0]

    def step(t, carry):
        current = []
        for x in range(local):
            block = recv_ref[pl.ds(t * tile, tile), x * capacity : (x + 1) * capacity, :]
            current.append(block.reshape(tile * capacity, block.shape[2]))
        at = pl.ds(pl.multiple_of(t * tile * capacity, tile * capacity), tile * capacity)
        for layer in range(layers):
            for x in range(local):
                weight = first_ref[x] if layer == 0 else hidden_ref[x, layer - 1]
                act, slope = layer_forward(dot(current[x], weight))
                act_ref[layer, x, at, :] = act
                slope_ref[layer, x, at, :] = slope
                current[x] = act
        raws = [dot_nt(head, current[x]) for x in range(local)]
        for s in range(tile):
            both = jnp.concatenate([r[:, s * capacity : (s + 1) * capacity] for r in raws], axis=0)
            held[pl.ds(pl.multiple_of((t * tile + s) * pairs, pairs), pairs), :] = both
        return carry

    lax.fori_loop(0, sources // tile, step, 0)
    raw = held[...].astype(BF16)
    for d in range(raw_ref.shape[0]):
        raw_ref[d] = raw


def composite(raw, spacing, bias, target):
    row, col = iota((LANES, LANES), 0), iota((LANES, LANES), 1)
    same = row // RAY_SAMPLES == col // RAY_SAMPLES

    def along(x, mask):
        high = x.astype(BF16)
        rest = x - high.astype(F32)
        mid = rest.astype(BF16)
        low = (rest - mid.astype(F32)).astype(BF16)
        w = hot(mask)
        return dot(high, w) + dot(mid, w) + dot(low, w)

    soft = jnp.maximum(raw[0], 0.0) + jnp.log1p(jnp.exp(-jnp.abs(raw[0])))
    optical = soft * spacing
    before = along(optical, same & (row < col))
    reach = jnp.exp(-before)
    left = jnp.exp(-optical)
    weight = reach * (1.0 - left)
    opacity = along(weight, same)
    rendered, graw = [], [None]
    pull = jnp.zeros_like(weight)
    for c in range(1, len(raw)):
        colour = jax.nn.sigmoid(raw[c] + bias[c - 1])
        shade = along(weight * colour, same) + (1.0 - opacity)
        off = shade - target[c - 1]
        rendered.append(shade)
        graw.append(off * weight * colour * (1.0 - colour))
        pull = pull + off * (colour - 1.0)
    optical_pull = pull * reach * left - along(pull * weight, same & (row > col))
    graw[0] = optical_pull * spacing * jax.nn.sigmoid(raw[0])
    return rendered, graw


def render_kernel(
    local, capacity, me_ref, meta_ref, raws_ref, act_ref, head_ref, gslot_ref, headpart_ref, rendered_ref, wide, ranked, dense, grad
):
    owners, pairs = raws_ref.shape[0], raws_ref.shape[1] // meta_ref.shape[0]
    sources = meta_ref.shape[0]
    experts = owners * local
    channels = pairs // local
    me = me_ref[0]
    wide[...] = raws_ref[...].astype(F32)
    samples = ranked.shape[2]
    chunks = samples // LANES
    member = iota((pairs, samples), 0) // channels

    def unslot(s, carry):
        region = meta_ref[s, :chunks, :].astype(F32).astype(jnp.int32)
        rank = lane_row(ranks(region, experts))
        name = lane_row(region)
        pick = hot(iota((capacity, samples), 0) == rank)
        ranked[s] = pick
        at = pl.ds(pl.multiple_of(s * pairs, pairs), pairs)
        block = wide[:, at, :].reshape(owners * pairs, capacity).astype(BF16)
        spread = dot(block, pick)
        total = jnp.zeros((pairs, samples), F32)
        for o in range(owners):
            total = total + jnp.where(name - o * local == member, spread[o * pairs : (o + 1) * pairs], 0.0)
        flat = total[:channels]
        for x in range(1, local):
            flat = flat + total[x * channels : (x + 1) * channels]
        for k in range(chunks):
            for c in range(channels):
                dense[c, pl.ds(s * chunks + k, 1), :] = flat[c : c + 1, k * LANES : (k + 1) * LANES]
        return carry

    lax.fori_loop(0, sources, unslot, 0)

    rays = samples // RAY_SAMPLES
    per_row = rays // chunks
    spacing = (meta_ref[:, chunks : 2 * chunks, :].astype(F32) + meta_ref[:, 2 * chunks : 3 * chunks, :].astype(F32)).reshape(
        sources * chunks, LANES
    )
    small = meta_ref[:, 3 * chunks :, :].astype(F32)
    belongs = iota((chunks, LANES), 1) % rays // per_row == iota((chunks, LANES), 0)
    belongs = belongs & (iota((chunks, LANES), 1) < 2 * rays)
    lay = hot(iota((LANES, LANES), 0) % per_row == iota((LANES, LANES), 1) // RAY_SAMPLES)
    laid = []
    for c in range(2 * (channels - 1)):
        rows = [jnp.where(belongs, small[s, c : c + 1, :], 0.0) for s in range(sources)]
        laid.append(dot(jnp.concatenate(rows, axis=0).astype(BF16), lay))
    shades, graw = composite(
        [dense[c] for c in range(channels)], spacing, laid[: channels - 1], laid[channels - 1 :]
    )
    for c in range(channels):
        grad[c] = graw[c]
    for c in range(channels - 1):
        wide_rows = shades[c].reshape(sources, chunks, LANES)
        mine = jnp.zeros((chunks, LANES), F32)
        for s in range(sources):
            mine = mine + jnp.where(me == s, wide_rows[s], 0.0)
        rendered_ref[c] = mine

    head_total = jnp.zeros((2 * channels, act_ref.shape[2]), F32)

    def slots(s, head_total):
        region = meta_ref[s, :chunks, :].astype(F32).astype(jnp.int32)
        name = lane_row(region)
        at = pl.ds(pl.multiple_of(s * chunks, chunks), chunks)
        flat = jnp.concatenate([lane_row(grad[c, at, :]) for c in range(channels)], axis=0)
        both = jnp.concatenate([flat] * local, axis=0)
        high, low = split(jnp.where(name - me * local == member, both, 0.0))
        got = dot_nt(jnp.concatenate([high, low], axis=0), ranked[s])
        for x in range(local):
            part = jnp.concatenate(
                [got[x * channels : (x + 1) * channels], got[pairs + x * channels : pairs + (x + 1) * channels]], axis=0
            ).astype(BF16)
            gslot_ref[x, s] = part
            feature = act_ref[x, pl.ds(pl.multiple_of(s * capacity, capacity), capacity), :]
            head_total = head_total + dot(part, feature)
        return head_total

    head_total = lax.fori_loop(0, sources, slots, head_total)
    part = head_total[:channels] + head_total[channels:]
    for d in range(headpart_ref.shape[0]):
        headpart_ref[d] = part


def backward_kernel(
    capacity, copies, me_ref, recv_ref, act_ref, slope_ref, gslot_ref, first_ref, hidden_ref, head_ref, *rest
):
    outs, (gfirst, ghidden) = rest[: 2 * copies], rest[2 * copies :]
    local, sources = gslot_ref.shape[0], gslot_ref.shape[1]
    layers = hidden_ref.shape[1] + 1
    head = head_ref[...]
    head = jnp.concatenate([head, head], axis=0)
    rows = sources * capacity
    up = []
    for x in range(local):
        pieces = [dot_tn(gslot_ref[x, s], head) for s in range(sources)]
        up.append(jnp.concatenate(pieces, axis=0).astype(BF16))
    for layer in reversed(range(layers)):
        for x in range(local):
            glin = up[x] * slope_ref[layer, x]
            if layer:
                ghidden[x, layer - 1] = dot_tn(act_ref[layer - 1, x], glin)
                up[x] = dot_nt(glin, hidden_ref[x, layer - 1]).astype(BF16)
            else:
                block = recv_ref[:, x * capacity : (x + 1) * capacity, :].reshape(rows, recv_ref.shape[2])
                gfirst[x] = dot_tn(block, glin)
    me = me_ref[0]
    for s in range(copies):
        first_out, hidden_out = outs[2 * s], outs[2 * s + 1]
        piece = lax.rem(me + s, copies)
        size = first_out.shape[1]
        first_out[...] = gfirst[:, pl.ds(pl.multiple_of(piece * size, size), size), :]
        size = hidden_out.shape[2]
        hidden_out[...] = ghidden[:, :, pl.ds(pl.multiple_of(piece * size, size), size), :]


def shape(dims, dtype):
    return jax.ShapeDtypeStruct(dims, dtype)


def call(kernel, outs, ins, scratch=(), scalars=0):
    specs = [pl.BlockSpec(memory_space=pltpu.SMEM)] * scalars
    specs += [pl.BlockSpec(memory_space=VMEM)] * (len(ins) - scalars)
    return pl.pallas_call(
        kernel,
        out_shape=outs,
        in_specs=specs,
        out_specs=[pl.BlockSpec(memory_space=VMEM)] * len(outs),
        scratch_shapes=list(scratch),
        compiler_params=pltpu.CompilerParams(vmem_limit_bytes=48 * 1024 * 1024),
    )(*ins)


def per_device(
    encoded, region_id, spacing, frame_index, target_rgb, frame_code, first_weight, hidden_weight, head_weight
):
    owners, copies = lax.axis_size("expert"), lax.axis_size("replica")
    local = first_weight.shape[0]
    experts = owners * local
    samples, enc_width = encoded.shape
    capacity = 2 * samples // experts
    hid = first_weight.shape[2]
    layers = hidden_weight.shape[1] + 1
    channels = head_weight.shape[0]
    chunks = samples // LANES
    slots = local * capacity
    rows = owners * capacity
    owner = lax.axis_index("expert").astype(jnp.int32).reshape(1)
    copy = lax.axis_index("replica").astype(jnp.int32).reshape(1)

    (outbound,) = call(
        functools.partial(dispatch_kernel, experts, capacity),
        [shape((owners, slots + META, enc_width), BF16)],
        [
            region_id.reshape(chunks, LANES),
            encoded,
            spacing.reshape(chunks, LANES),
            frame_index.reshape(1, -1),
            target_rgb,
            frame_code,
        ],
    )
    recv = lax.all_to_all(outbound, "expert", split_axis=0, concat_axis=0, tiled=True)
    rows_out = owners * local * channels
    acts, slopes, raw = call(
        functools.partial(forward_kernel, capacity, 2),
        [
            shape((layers, local, rows, hid), BF16),
            shape((layers, local, rows, hid), BF16),
            shape((owners, rows_out, capacity), BF16),
        ],
        [recv, first_weight, hidden_weight, head_weight],
        [pltpu.VMEM((rows_out, capacity), F32)],
    )
    raws = lax.all_to_all(raw, "expert", split_axis=0, concat_axis=0, tiled=True)
    meta = recv[:, slots:, :]
    gslot, headpart, rendered = call(
        functools.partial(render_kernel, local, capacity),
        [
            shape((local, owners, 2 * channels, capacity), BF16),
            shape((owners * copies, channels, hid), F32),
            shape((channels - 1, chunks, LANES), F32),
        ],
        [owner, meta, raws, acts[layers - 1], head_weight],
        [
            pltpu.VMEM((owners, owners * local * channels, capacity), F32),
            pltpu.VMEM((owners, capacity, samples), BF16),
            pltpu.VMEM((channels, owners * chunks, LANES), F32),
            pltpu.VMEM((channels, owners * chunks, LANES), F32),
        ],
        scalars=1,
    )
    heads = lax.all_to_all(headpart, ("expert", "replica"), split_axis=0, concat_axis=0, tiled=True)
    pieces = []
    for _ in range(copies):
        pieces.append(shape((local, enc_width // copies, hid), F32))
        pieces.append(shape((local, layers - 1, hid // copies, hid), F32))
    grads = call(
        functools.partial(backward_kernel, capacity, copies),
        pieces,
        [copy, recv, acts, slopes, gslot, first_weight, hidden_weight, head_weight],
        [pltpu.VMEM(first_weight.shape, F32), pltpu.VMEM(hidden_weight.shape, F32)],
        scalars=1,
    )
    first_grad, hidden_grad = grads[0], grads[1]
    for s in range(1, copies):
        ring = [(i, (i + s) % copies) for i in range(copies)]
        first_grad = first_grad + lax.ppermute(grads[2 * s], "replica", ring)
        hidden_grad = hidden_grad + lax.ppermute(grads[2 * s + 1], "replica", ring)
    head_grad = jnp.sum(heads, axis=0)
    rendered = rendered[:, :, ::RAY_SAMPLES].reshape(channels - 1, -1)
    return (first_grad, hidden_grad, head_grad, rendered)


def solution(mesh):
    placed = (
        P(("groups", "expert", "replica"), None),
        P(("groups", "expert", "replica")),
        P(("groups", "expert", "replica")),
        P(("groups", "expert", "replica")),
        P(None, ("groups", "expert", "replica")),
        P(None, "groups"),
        P("expert", None, None),
        P("expert", None, None, None),
        P(),
    )
    return jax.shard_map(
        per_device,
        mesh=mesh,
        in_specs=placed,
        out_specs=(
            P(("groups", "expert"), "replica", None),
            P(("groups", "expert"), None, "replica", None),
            P("groups", None),
            P(None, ("groups", "expert", "replica")),
        ),
        check_vma=False,
    )
```

```python
import functools

import jax
import jax.numpy as jnp
from jax import lax
from jax.experimental import pallas as pl
from jax.experimental.pallas import tpu as pltpu
from jax.sharding import PartitionSpec as P

RAY_SAMPLES = 64
LANES = 128
META = 32
F32 = jnp.float32
BF16 = jnp.bfloat16
VMEM = pltpu.VMEM


def iota(shape, dim):
    return lax.broadcasted_iota(jnp.int32, shape, dim)


def hot(mask, dtype=BF16):
    return jnp.where(mask, 1.0, 0.0).astype(dtype)


def dot(a, b):
    return jnp.dot(a, b, preferred_element_type=F32)


def dot_nt(a, b):
    return lax.dot_general(a, b, (((1,), (1,)), ((), ())), preferred_element_type=F32)


def dot_tn(a, b):
    return lax.dot_general(a, b, (((0,), (0,)), ((), ())), preferred_element_type=F32)


def split(x):
    high = x.astype(BF16)
    return high, (x - high.astype(F32)).astype(BF16)


def lane_row(x):
    return jnp.concatenate([x[k : k + 1] for k in range(x.shape[0])], axis=1)


def ranks(region, experts):
    rows = region.shape[0]
    names = iota((experts, LANES), 0)
    upper = hot(iota((LANES, LANES), 0) <= iota((LANES, LANES), 1))
    equal = [hot(region[k : k + 1] == names, F32) for k in range(rows)]
    running = dot(jnp.concatenate(equal, axis=0).astype(BF16), upper)
    before = jnp.zeros((experts, 1), F32)
    out = []
    for k in range(rows):
        here = running[k * experts : (k + 1) * experts]
        out.append(jnp.sum(equal[k] * (here + before), axis=0, keepdims=True))
        before = before + here[:, LANES - 1 :]
    return jnp.concatenate(out, axis=0).astype(jnp.int32) - 1


def dispatch_kernel(experts, capacity, *refs):
    outside, (out_ref, first_out, hidden_out, head_out), refs = refs[:9], refs[9:13], refs[13:]
    inside, (held, loaded, sent) = refs[:9], refs[9:]
    loads = [pltpu.make_async_copy(a, b, loaded.at[i]) for i, (a, b) in enumerate(zip(outside, inside))]
    for load in loads:
        load.start()
    region_ref, enc_ref, spacing_ref, frame_ref, target_ref, code_ref, first_ref, hidden_ref, head_ref = inside
    owners, rows = held.shape[0], held.shape[1] - META
    samples = enc_ref.shape[0]
    for load in loads[:6]:
        load.wait()
    region = region_ref[...]
    slot = lane_row(region * capacity + ranks(region, experts))
    enc = enc_ref[...]

    frames = code_ref.shape[1]
    rays = frame_ref.shape[1]
    chosen = hot(frame_ref[...] == iota((frames, rays), 0), F32)
    bias = lax.dot_general(
        code_ref[...], chosen, (((1,), (0,)), ((), ())), precision=lax.Precision.HIGHEST, preferred_element_type=F32
    )
    small = jnp.concatenate([bias, target_ref[...], jnp.zeros((2, rays), F32)], axis=0)
    small_high, small_low = split(small)
    small = jnp.concatenate(
        [small_high.astype(F32), small_low.astype(F32), jnp.zeros((8, LANES - 2 * rays), F32)], axis=1
    )
    spacing_high, spacing_low = split(spacing_ref[...])
    meta = jnp.concatenate(
        [region.astype(F32), spacing_high.astype(F32), spacing_low.astype(F32), small], axis=0
    ).astype(BF16)

    def send(d):
        return pltpu.make_async_copy(held.at[d], out_ref.at[d], sent.at[d])

    def one(d, carry):
        pick = hot(iota((rows, samples), 0) == slot - d * rows)
        held[d, :rows, :] = dot(pick, enc).astype(BF16)
        held[d, rows:, :] = meta
        send(d).start()
        return carry

    lax.fori_loop(0, owners, one, 0, unroll=2)
    for load in loads[6:]:
        load.wait()
    first_out[...] = first_ref[...] * 0.5
    hidden_out[...] = hidden_ref[...] * 0.5
    head_out[...] = head_ref[...]

    def finish(d, carry):
        send(d).wait()
        return carry

    lax.fori_loop(0, owners, finish, 0)


def layer_forward(half):
    t = jnp.tanh(half)
    p = half * t
    return (half + p).astype(BF16), ((1.0 + t) * (1.0 + (half - p))).astype(BF16)


def forward_kernel(
    capacity, tile, recv_ref, first_ref, hidden_ref, head_ref, act_out, slope_out, raw_ref, top_ref, held, act_ref, slope_ref, done
):
    sources = recv_ref.shape[0]
    local = first_ref.shape[0]
    layers = hidden_ref.shape[1] + 1
    head = head_ref[...]
    pairs = local * head.shape[0]

    def saves(t):
        at = pl.ds(pl.multiple_of(t * tile * capacity, tile * capacity), tile * capacity)
        return (
            pltpu.make_async_copy(act_ref.at[:, :, at, :], act_out.at[:, :, at, :], done.at[0, t]),
            pltpu.make_async_copy(slope_ref.at[:, :, at, :], slope_out.at[:, :, at, :], done.at[1, t]),
        )

    def step(t, carry):
        current = []
        for x in range(local):
            block = recv_ref[pl.ds(t * tile, tile), x * capacity : (x + 1) * capacity, :]
            current.append(block.reshape(tile * capacity, block.shape[2]))
        at = pl.ds(pl.multiple_of(t * tile * capacity, tile * capacity), tile * capacity)
        for layer in range(layers):
            for x in range(local):
                weight = first_ref[x] if layer == 0 else hidden_ref[x, layer - 1]
                act, slope = layer_forward(dot(current[x], weight))
                if layer < layers - 1:
                    act_ref[layer, x, at, :] = act
                else:
                    top_ref[x, at, :] = act
                slope_ref[layer, x, at, :] = slope
                current[x] = act
        raws = [dot_nt(head, current[x]) for x in range(local)]
        for s in range(tile):
            both = jnp.concatenate([r[:, s * capacity : (s + 1) * capacity] for r in raws], axis=0)
            held[pl.ds(pl.multiple_of((t * tile + s) * pairs, pairs), pairs), :] = both
        for save in saves(t):
            save.start()
        return carry

    lax.fori_loop(0, sources // tile, step, 0)
    raw = held[...].astype(BF16)
    for d in range(raw_ref.shape[0]):
        raw_ref[d] = raw

    def finish(t, carry):
        for save in saves(t):
            save.wait()
        return carry

    lax.fori_loop(0, sources // tile, finish, 0)


def composite(raw, spacing, bias, target):
    row, col = iota((LANES, LANES), 0), iota((LANES, LANES), 1)
    same = row // RAY_SAMPLES == col // RAY_SAMPLES

    def along(x, mask):
        high = x.astype(BF16)
        rest = x - high.astype(F32)
        mid = rest.astype(BF16)
        low = (rest - mid.astype(F32)).astype(BF16)
        w = hot(mask)
        return dot(high, w) + dot(mid, w) + dot(low, w)

    soft = jnp.maximum(raw[0], 0.0) + jnp.log1p(jnp.exp(-jnp.abs(raw[0])))
    optical = soft * spacing
    before = along(optical, same & (row < col))
    reach = jnp.exp(-before)
    left = jnp.exp(-optical)
    weight = reach * (1.0 - left)
    opacity = along(weight, same)
    rendered, graw = [], [None]
    pull = jnp.zeros_like(weight)
    for c in range(1, len(raw)):
        colour = jax.nn.sigmoid(raw[c] + bias[c - 1])
        shade = along(weight * colour, same) + (1.0 - opacity)
        off = shade - target[c - 1]
        rendered.append(shade)
        graw.append(off * weight * colour * (1.0 - colour))
        pull = pull + off * (colour - 1.0)
    optical_pull = pull * reach * left - along(pull * weight, same & (row > col))
    graw[0] = optical_pull * spacing * jax.nn.sigmoid(raw[0])
    return rendered, graw


def plan_kernel(
    local, capacity, act_in, recv_ref, actt_out, rank_ref, name_ref, laid_ref, enct_ref, act_ref, actt_ref, moved
):
    layers = actt_ref.shape[0]
    loads = [pltpu.make_async_copy(act_in.at[k], act_ref.at[k], moved.at[0, k]) for k in range(layers)]
    saves = [pltpu.make_async_copy(actt_ref.at[k], actt_out.at[k], moved.at[1, k]) for k in range(layers)]
    for load in loads:
        load.start()
    sources, slots = recv_ref.shape[0], recv_ref.shape[1] - META
    rows = sources * capacity
    experts = sources * local
    samples = rank_ref.shape[2]
    chunks = samples // LANES

    def one(s, carry):
        region = recv_ref[s, slots : slots + chunks, :].astype(F32).astype(jnp.int32)
        rank_ref[s] = jnp.broadcast_to(lane_row(ranks(region, experts)), (8, samples))
        name_ref[s] = jnp.broadcast_to(lane_row(region), (8, samples))
        return carry

    lax.fori_loop(0, sources, one, 0, unroll=2)

    rays = samples // RAY_SAMPLES
    per_row = rays // chunks
    meta = recv_ref[:, slots:, :].astype(F32)
    laid_ref[0] = (meta[:, chunks : 2 * chunks] + meta[:, 2 * chunks : 3 * chunks]).reshape(sources * chunks, LANES)
    small = meta[:, 3 * chunks :]
    lane = iota((chunks, LANES), 1)
    belongs = (lane % rays // per_row == iota((chunks, LANES), 0)) & (lane < 2 * rays)
    lay = hot(iota((LANES, LANES), 0) % per_row == iota((LANES, LANES), 1) // RAY_SAMPLES)
    for c in range(laid_ref.shape[0] - 1):
        parts = [jnp.where(belongs, small[s, c : c + 1, :], 0.0) for s in range(sources)]
        laid_ref[1 + c] = dot(jnp.concatenate(parts, axis=0).astype(BF16), lay)

    for x in range(local):
        enct_ref[x] = recv_ref[:, x * capacity : (x + 1) * capacity, :].reshape(rows, recv_ref.shape[2]).T
    for layer in reversed(range(layers)):
        loads[layer].wait()
        for x in range(local):
            actt_ref[layer, x] = act_ref[layer, x].T
        saves[layer].start()
    for save in saves:
        save.wait()


def render_kernel(
    local,
    capacity,
    me_ref,
    act_ref,
    raws_ref,
    rank_ref,
    name_ref,
    laid_ref,
    gslot_ref,
    headpart_ref,
    rendered_ref,
    wide,
    dense,
    grad,
    ranked_ref,
):
    sources, samples = ranked_ref.shape[0], ranked_ref.shape[2]
    owners, pairs = raws_ref.shape[0], raws_ref.shape[1] // sources
    channels = pairs // local
    me = me_ref[0]
    wide[...] = raws_ref[...].astype(F32)
    chunks = samples // LANES
    member = iota((pairs, samples), 0) // channels

    def unslot(s, carry):
        name = name_ref[s, :pairs, :]
        at = pl.ds(pl.multiple_of(s * pairs, pairs), pairs)
        block = wide[:, at, :].reshape(owners * pairs, capacity).astype(BF16)
        pick = hot(iota((capacity, samples), 0) == rank_ref[s, :1, :])
        ranked_ref[s] = pick
        spread = dot(block, pick)
        total = jnp.zeros((pairs, samples), F32)
        for o in range(owners):
            total = total + jnp.where(name - o * local == member, spread[o * pairs : (o + 1) * pairs], 0.0)
        flat = total[:channels]
        for x in range(1, local):
            flat = flat + total[x * channels : (x + 1) * channels]
        for k in range(chunks):
            for c in range(channels):
                dense[c, pl.ds(s * chunks + k, 1), :] = flat[c : c + 1, k * LANES : (k + 1) * LANES]
        return carry

    lax.fori_loop(0, sources, unslot, 0, unroll=4)

    shades, graw = composite(
        [dense[c] for c in range(channels)],
        laid_ref[0],
        [laid_ref[c] for c in range(1, channels)],
        [laid_ref[c] for c in range(channels, 2 * channels - 1)],
    )
    for c in range(channels):
        grad[c] = graw[c]
    for c in range(channels - 1):
        dense[c] = shades[c]
        rendered_ref[c] = dense[c, pl.ds(pl.multiple_of(me * chunks, chunks), chunks), :]

    parts = [[] for _ in range(local)]
    for s in range(sources):
        own = name_ref[s, :pairs, :] - me * local == member
        flat = jnp.concatenate([lane_row(grad[c, s * chunks : (s + 1) * chunks, :]) for c in range(channels)], axis=0)
        high, low = split(jnp.where(own, jnp.concatenate([flat] * local, axis=0), 0.0))
        got = dot_nt(jnp.concatenate([high, low], axis=0), ranked_ref[s])
        for x in range(local):
            parts[x].append(
                jnp.concatenate(
                    [got[x * channels : (x + 1) * channels], got[pairs + x * channels : pairs + (x + 1) * channels]],
                    axis=0,
                )
            )
    head_total = None
    for x in range(local):
        part = jnp.concatenate(parts[x], axis=1).astype(BF16)
        gslot_ref[x] = part
        add = dot(part, act_ref[x])
        head_total = add if head_total is None else head_total + add
    head_total = head_total[:channels] + head_total[channels:]
    for d in range(headpart_ref.shape[0]):
        headpart_ref[d] = head_total


def backward_kernel(copies, me_ref, slope_in, actt_in, gslot_ref, enct_ref, hidden_ref, head_ref, *rest):
    outs, (gfirst, ghidden, slope_ref, actt_ref, moved) = rest[: 2 * copies], rest[2 * copies :]
    local = gslot_ref.shape[0]
    layers = hidden_ref.shape[1] + 1
    loads = []
    for layer in range(layers):
        some = [pltpu.make_async_copy(slope_in.at[layer], slope_ref.at[layer], moved.at[0, layer])]
        if layer:
            some.append(pltpu.make_async_copy(actt_in.at[layer - 1], actt_ref.at[layer - 1], moved.at[1, layer]))
        loads.append(some)
    for some in reversed(loads):
        for load in some:
            load.start()
    head = head_ref[...] * 0.5
    head = jnp.concatenate([head, head], axis=0)
    up = [dot_tn(gslot_ref[x], head).astype(BF16) for x in range(local)]
    for layer in reversed(range(layers)):
        for load in loads[layer]:
            load.wait()
        for x in range(local):
            glin = up[x] * slope_ref[layer, x]
            if layer:
                ghidden[x, layer - 1] = dot(actt_ref[layer - 1, x], glin)
                up[x] = dot_nt(glin, hidden_ref[x, layer - 1]).astype(BF16)
            else:
                gfirst[x] = dot(enct_ref[x], glin)
    me = me_ref[0]
    for s in range(copies):
        first_out, hidden_out = outs[2 * s], outs[2 * s + 1]
        piece = lax.rem(me + s, copies)
        size = first_out.shape[1]
        first_out[...] = gfirst[:, pl.ds(pl.multiple_of(piece * size, size), size), :]
        size = hidden_out.shape[2]
        hidden_out[...] = ghidden[:, :, pl.ds(pl.multiple_of(piece * size, size), size), :]


def head_kernel(heads_ref, out_ref):
    out_ref[...] = jnp.sum(heads_ref[...], axis=0)


def sum_kernel(copies, head_ref, *refs):
    pieces, outs, (first_ref, hidden_ref, done) = refs[: 2 * copies], refs[2 * copies : 2 * copies + 2], refs[2 * copies + 2 :]
    for k, held in enumerate((hidden_ref, first_ref)):
        total = pieces[1 - k][...]
        for s in range(1, copies):
            total = total + pieces[2 * s + 1 - k][...]
        held[...] = total
        pltpu.make_async_copy(held, outs[1 - k], done.at[k]).start()
    for k, held in enumerate((hidden_ref, first_ref)):
        pltpu.make_async_copy(held, outs[1 - k], done.at[k]).wait()


def shape(dims, dtype):
    return jax.ShapeDtypeStruct(dims, dtype)


def call(kernel, outs, ins, scratch=(), scalars=0, outside=(0, 0), flops=0, limit=24, pinned=True):
    specs = [pl.BlockSpec(memory_space=pltpu.SMEM)] * scalars
    specs += [pl.BlockSpec(memory_space=pl.ANY)] * outside[0]
    specs += [pl.BlockSpec(memory_space=VMEM)] * (len(ins) - len(specs))
    out_specs = [pl.BlockSpec(memory_space=pl.ANY)] * outside[1]
    out_specs += [pl.BlockSpec(memory_space=VMEM)] * (len(outs) - len(out_specs))
    held = [
        x if i < scalars else pltpu.with_memory_space_constraint(x, pltpu.HBM if i < scalars + outside[0] else VMEM)
        for i, x in enumerate(ins)
    ]
    return pl.pallas_call(
        kernel,
        out_shape=[
            (pltpu.HBM if i < outside[1] else VMEM)(x.shape, x.dtype) if pinned else x for i, x in enumerate(outs)
        ],
        in_specs=specs,
        out_specs=out_specs,
        scratch_shapes=list(scratch),
        cost_estimate=pl.CostEstimate(flops=flops, bytes_accessed=0, transcendentals=0),
        compiler_params=pltpu.CompilerParams(vmem_limit_bytes=limit * 1024 * 1024),
    )(*held)


def per_device(
    encoded, region_id, spacing, frame_index, target_rgb, frame_code, first_weight, hidden_weight, head_weight
):
    owners, copies = lax.axis_size("expert"), lax.axis_size("replica")
    local = first_weight.shape[0]
    experts = owners * local
    samples, enc_width = encoded.shape
    capacity = 2 * samples // experts
    hid = first_weight.shape[2]
    layers = hidden_weight.shape[1] + 1
    channels = head_weight.shape[0]
    chunks = samples // LANES
    slots = local * capacity
    rows = owners * capacity
    owner = lax.axis_index("expert").astype(jnp.int32).reshape(1)
    copy = lax.axis_index("replica").astype(jnp.int32).reshape(1)

    inputs = [
        region_id.reshape(chunks, LANES),
        encoded,
        spacing.reshape(chunks, LANES),
        frame_index.reshape(1, -1),
        target_rgb,
        frame_code,
        first_weight,
        hidden_weight,
        head_weight,
    ]
    outbound, first_half, hidden_half, head = call(
        functools.partial(dispatch_kernel, experts, capacity),
        [
            shape((owners, slots + META, enc_width), BF16),
            shape(first_weight.shape, BF16),
            shape(hidden_weight.shape, BF16),
            shape(head_weight.shape, BF16),
        ],
        inputs,
        [pltpu.VMEM(x.shape, x.dtype) for x in inputs]
        + [
            pltpu.VMEM((owners, slots + META, enc_width), BF16),
            pltpu.SemaphoreType.DMA((len(inputs),)),
            pltpu.SemaphoreType.DMA((owners,)),
        ],
        outside=(len(inputs), 1),
    )
    recv = lax.all_to_all(outbound, "expert", split_axis=0, concat_axis=0, tiled=True)
    pairs = local * channels
    big = (layers, local, rows, hid)
    tile = 2
    acts, slopes, raw, top = call(
        functools.partial(forward_kernel, capacity, tile),
        [
            shape((layers - 1, local, rows, hid), BF16),
            shape(big, BF16),
            shape((owners, owners * pairs, capacity), BF16),
            shape((local, rows, hid), BF16),
        ],
        [recv, first_half, hidden_half, head],
        [
            pltpu.VMEM((owners * pairs, capacity), F32),
            pltpu.VMEM((layers - 1, local, rows, hid), BF16),
            pltpu.VMEM(big, BF16),
            pltpu.SemaphoreType.DMA((2, owners // tile)),
        ],
        outside=(0, 2),
        flops=10**9,
    )
    raws = lax.all_to_all(raw, "expert", split_axis=0, concat_axis=0, tiled=True)
    flipped = (layers - 1, local, hid, rows)
    actt, order, names, laid, enct = call(
        functools.partial(plan_kernel, local, capacity),
        [
            shape(flipped, BF16),
            shape((owners, 8, samples), jnp.int32),
            shape((owners, 8, samples), jnp.int32),
            shape((2 * channels - 1, owners * chunks, LANES), F32),
            shape((local, enc_width, rows), BF16),
        ],
        [acts, recv],
        [
            pltpu.VMEM((layers - 1, local, rows, hid), BF16),
            pltpu.VMEM(flipped, BF16),
            pltpu.SemaphoreType.DMA((2, layers - 1)),
        ],
        outside=(1, 1),
        flops=5 * 10**9,
    )
    gslot, headpart, rendered = call(
        functools.partial(render_kernel, local, capacity),
        [
            shape((local, 2 * channels, rows), BF16),
            shape((owners * copies, channels, hid), F32),
            shape((channels - 1, chunks, LANES), F32),
        ],
        [owner, top, raws, order, names, laid],
        [
            pltpu.VMEM((owners, owners * pairs, capacity), F32),
            pltpu.VMEM((channels, owners * chunks, LANES), F32),
            pltpu.VMEM((channels, owners * chunks, LANES), F32),
            pltpu.VMEM((owners, capacity, samples), BF16),
        ],
        scalars=1,
        flops=10**9,
    )
    heads = lax.all_to_all(headpart, ("expert", "replica"), split_axis=0, concat_axis=0, tiled=True)
    pieces = []
    for _ in range(copies):
        pieces.append(shape((local, enc_width // copies, hid), F32))
        pieces.append(shape((local, layers - 1, hid // copies, hid), F32))
    grads = call(
        functools.partial(backward_kernel, copies),
        pieces,
        [copy, slopes, actt, gslot, enct, hidden_half, head],
        [
            pltpu.VMEM(first_weight.shape, F32),
            pltpu.VMEM(hidden_weight.shape, F32),
            pltpu.VMEM(big, BF16),
            pltpu.VMEM(flipped, BF16),
            pltpu.SemaphoreType.DMA((2, layers)),
        ],
        scalars=1,
        outside=(2, 0),
        flops=5 * 10**9,
    )
    grads = list(grads)
    for s in range(1, copies):
        ring = [(i, (i + s) % copies) for i in range(copies)]
        for k in (2 * s, 2 * s + 1):
            grads[k] = lax.ppermute(grads[k], "replica", ring)
    (head_grad,) = call(head_kernel, [shape((channels, hid), F32)], [heads], flops=10**11, pinned=False)
    first_grad, hidden_grad = call(
        functools.partial(sum_kernel, copies),
        [shape(grads[0].shape, F32), shape(grads[1].shape, F32)],
        [head_grad, *grads],
        [pltpu.VMEM(grads[0].shape, F32), pltpu.VMEM(grads[1].shape, F32), pltpu.SemaphoreType.DMA((2,))],
        outside=(1, 2),
    )
    rendered = rendered[:, :, ::RAY_SAMPLES].reshape(channels - 1, -1)
    return (first_grad, hidden_grad, head_grad, rendered)


def solution(mesh):
    placed = (
        P(("groups", "expert", "replica"), None),
        P(("groups", "expert", "replica")),
        P(("groups", "expert", "replica")),
        P(("groups", "expert", "replica")),
        P(None, ("groups", "expert", "replica")),
        P(None, "groups"),
        P("expert", None, None),
        P("expert", None, None, None),
        P(),
    )
    return jax.shard_map(
        per_device,
        mesh=mesh,
        in_specs=placed,
        out_specs=(
            P(("groups", "expert"), "replica", None),
            P(("groups", "expert"), None, "replica", None),
            P("groups", None),
            P(None, ("groups", "expert", "replica")),
        ),
        check_vma=False,
    )
```

```python
import functools

import jax
import jax.numpy as jnp
from jax import lax
from jax.experimental import pallas as pl
from jax.experimental.pallas import tpu as pltpu
from jax.sharding import PartitionSpec as P

RAY_SAMPLES = 64
LANES = 128
META = 32
F32 = jnp.float32
BF16 = jnp.bfloat16
VMEM = pltpu.VMEM


def iota(shape, dim):
    return lax.broadcasted_iota(jnp.int32, shape, dim)


def hot(mask, dtype=BF16):
    return jnp.where(mask, 1.0, 0.0).astype(dtype)


def dot(a, b):
    return jnp.dot(a, b, preferred_element_type=F32)


def dot_nt(a, b):
    return lax.dot_general(a, b, (((1,), (1,)), ((), ())), preferred_element_type=F32)


def dot_tn(a, b):
    return lax.dot_general(a, b, (((0,), (0,)), ((), ())), preferred_element_type=F32)


def split(x):
    high = x.astype(BF16)
    return high, (x - high.astype(F32)).astype(BF16)


def lane_row(x):
    return jnp.concatenate([x[k : k + 1] for k in range(x.shape[0])], axis=1)


def ranks(region, experts):
    rows = region.shape[0]
    names = iota((experts, LANES), 0)
    upper = hot(iota((LANES, LANES), 0) <= iota((LANES, LANES), 1))
    equal = [hot(region[k : k + 1] == names, F32) for k in range(rows)]
    running = dot(jnp.concatenate(equal, axis=0).astype(BF16), upper)
    before = jnp.zeros((experts, 1), F32)
    out = []
    for k in range(rows):
        here = running[k * experts : (k + 1) * experts]
        out.append(jnp.sum(equal[k] * (here + before), axis=0, keepdims=True))
        before = before + here[:, LANES - 1 :]
    return jnp.concatenate(out, axis=0).astype(jnp.int32) - 1


def dispatch_kernel(experts, capacity, *refs):
    outside, out_ref, inside, (held, loaded, sent) = refs[:6], refs[6], refs[7:13], refs[13:]
    loads = [pltpu.make_async_copy(a, b, loaded.at[i]) for i, (a, b) in enumerate(zip(outside, inside))]
    for load in loads:
        load.start()
    region_ref, enc_ref, spacing_ref, frame_ref, target_ref, code_ref = inside
    owners, rows = held.shape[0], held.shape[1] - META
    samples = enc_ref.shape[0]
    for load in loads:
        load.wait()
    region = region_ref[...]
    slot = lane_row(region * capacity + ranks(region, experts))
    enc = enc_ref[...]

    frames = code_ref.shape[1]
    rays = frame_ref.shape[1]
    chosen = hot(frame_ref[...] == iota((frames, rays), 0), F32)
    bias = lax.dot_general(
        code_ref[...], chosen, (((1,), (0,)), ((), ())), precision=lax.Precision.HIGHEST, preferred_element_type=F32
    )
    small = jnp.concatenate([bias, target_ref[...], jnp.zeros((2, rays), F32)], axis=0)
    small_high, small_low = split(small)
    small = jnp.concatenate(
        [small_high.astype(F32), small_low.astype(F32), jnp.zeros((8, LANES - 2 * rays), F32)], axis=1
    )
    spacing_high, spacing_low = split(spacing_ref[...])
    meta = jnp.concatenate(
        [region.astype(F32), spacing_high.astype(F32), spacing_low.astype(F32), small], axis=0
    ).astype(BF16)

    def send(d):
        return pltpu.make_async_copy(held.at[d], out_ref.at[d], sent.at[d])

    def one(d, carry):
        pick = hot(iota((rows, samples), 0) == slot - d * rows)
        held[d, :rows, :] = dot(pick, enc).astype(BF16)
        held[d, rows:, :] = meta
        send(d).start()
        return carry

    lax.fori_loop(0, owners, one, 0, unroll=8)

    def finish(d, carry):
        send(d).wait()
        return carry

    lax.fori_loop(0, owners, finish, 0)


def weight_kernel(first_in, hidden_in, head_in, first_out, hidden_out, head_out, first_ref, hidden_ref, moved):
    loads = [
        pltpu.make_async_copy(first_in, first_ref, moved.at[0]),
        pltpu.make_async_copy(hidden_in, hidden_ref, moved.at[1]),
        pltpu.make_async_copy(head_in, head_out, moved.at[2]),
    ]
    for load in loads:
        load.start()
    for load in loads:
        load.wait()
    first_out[...] = first_ref[...] * 0.5
    hidden_out[...] = hidden_ref[...] * 0.5


def layer_forward(half):
    t = jnp.tanh(half)
    p = half * t
    return (half + p).astype(BF16), ((1.0 + t) * (1.0 + (half - p))).astype(BF16)


def forward_kernel(
    capacity,
    tile,
    recv_ref,
    first_ref,
    hidden_ref,
    head_ref,
    act_out,
    slope_out,
    raw_ref,
    act_top,
    held,
    act_ref,
    slope_ref,
    done,
):
    sources = recv_ref.shape[0]
    local = first_ref.shape[0]
    layers = hidden_ref.shape[1] + 1
    head = head_ref[...]
    pairs = local * head.shape[0]

    def rows_of(t):
        return pl.ds(pl.multiple_of(t * tile * capacity, tile * capacity), tile * capacity)

    def saves(t, layer):
        at = rows_of(t)
        pairs_of = [(slope_ref, slope_out)] + ([(act_ref, act_out)] if layer < layers - 1 else [])
        return [
            pltpu.make_async_copy(a.at[layer, :, at, :], b.at[layer, :, at, :], done.at[k, layer, t])
            for k, (a, b) in enumerate(pairs_of)
        ]

    def step(t, carry):
        current = []
        for x in range(local):
            block = recv_ref[pl.ds(t * tile, tile), x * capacity : (x + 1) * capacity, :]
            current.append(block.reshape(tile * capacity, block.shape[2]))
        at = rows_of(t)
        for layer in range(layers):
            for x in range(local):
                weight = first_ref[x] if layer == 0 else hidden_ref[x, layer - 1]
                act, slope = layer_forward(dot(current[x], weight))
                slope_ref[layer, x, at, :] = slope
                if layer < layers - 1:
                    act_ref[layer, x, at, :] = act
                else:
                    act_top[x, at, :] = act
                current[x] = act
            for save in saves(t, layer):
                save.start()
        raws = [dot_nt(head, current[x]) for x in range(local)]
        for s in range(tile):
            both = jnp.concatenate([r[:, s * capacity : (s + 1) * capacity] for r in raws], axis=0)
            held[pl.ds(pl.multiple_of((t * tile + s) * pairs, pairs), pairs), :] = both
        return carry

    lax.fori_loop(0, sources // tile, step, 0)
    raw = held[...].astype(BF16)
    for d in range(raw_ref.shape[0]):
        raw_ref[d] = raw

    def finish(t, carry):
        for layer in range(layers):
            for save in saves(t, layer):
                save.wait()
        return carry

    lax.fori_loop(0, sources // tile, finish, 0)


def composite(raw, spacing, bias, target):
    row, col = iota((LANES, LANES), 0), iota((LANES, LANES), 1)
    same = row // RAY_SAMPLES == col // RAY_SAMPLES

    def along(x, mask):
        high = x.astype(BF16)
        rest = x - high.astype(F32)
        mid = rest.astype(BF16)
        low = (rest - mid.astype(F32)).astype(BF16)
        w = hot(mask)
        return dot(high, w) + dot(mid, w) + dot(low, w)

    soft = jnp.maximum(raw[0], 0.0) + jnp.log1p(jnp.exp(-jnp.abs(raw[0])))
    optical = soft * spacing
    before = along(optical, same & (row < col))
    reach = jnp.exp(-before)
    left = jnp.exp(-optical)
    weight = reach * (1.0 - left)
    opacity = along(weight, same)
    rendered, graw = [], [None]
    pull = jnp.zeros_like(weight)
    for c in range(1, len(raw)):
        colour = jax.nn.sigmoid(raw[c] + bias[c - 1])
        shade = along(weight * colour, same) + (1.0 - opacity)
        off = shade - target[c - 1]
        rendered.append(shade)
        graw.append(off * weight * colour * (1.0 - colour))
        pull = pull + off * (colour - 1.0)
    optical_pull = pull * reach * left - along(pull * weight, same & (row > col))
    graw[0] = optical_pull * spacing * jax.nn.sigmoid(raw[0])
    return rendered, graw


def plan_kernel(
    local, capacity, act_in, recv_ref, actt_out, enct_out, rank_ref, name_ref, laid_ref, act_ref, actt_ref, enct_ref, moved
):
    layers = actt_ref.shape[0]
    loads = [pltpu.make_async_copy(act_in.at[k], act_ref.at[k], moved.at[0, k]) for k in range(layers)]
    saves = [pltpu.make_async_copy(actt_ref.at[k], actt_out.at[k], moved.at[1, k]) for k in range(layers)]
    for load in loads:
        load.start()
    sources, slots = recv_ref.shape[0], recv_ref.shape[1] - META
    rows = sources * capacity
    experts = sources * local
    samples = rank_ref.shape[1]
    chunks = samples // LANES

    def one(s, carry):
        region = recv_ref[s, slots : slots + chunks, :].astype(F32).astype(jnp.int32)
        rank_ref[pl.ds(s, 1), :] = lane_row(ranks(region, experts))
        name_ref[pl.ds(s, 1), :] = lane_row(region)
        return carry

    lax.fori_loop(0, sources, one, 0, unroll=2)

    rays = samples // RAY_SAMPLES
    per_row = rays // chunks
    meta = recv_ref[:, slots:, :].astype(F32)
    laid_ref[0] = (meta[:, chunks : 2 * chunks] + meta[:, 2 * chunks : 3 * chunks]).reshape(sources * chunks, LANES)
    small = meta[:, 3 * chunks :]
    lane = iota((chunks, LANES), 1)
    belongs = (lane % rays // per_row == iota((chunks, LANES), 0)) & (lane < 2 * rays)
    lay = hot(iota((LANES, LANES), 0) % per_row == iota((LANES, LANES), 1) // RAY_SAMPLES)
    for c in range(laid_ref.shape[0] - 1):
        parts = [jnp.where(belongs, small[s, c : c + 1, :], 0.0) for s in range(sources)]
        laid_ref[1 + c] = dot(jnp.concatenate(parts, axis=0).astype(BF16), lay)

    for x in range(local):
        enct_ref[x] = recv_ref[:, x * capacity : (x + 1) * capacity, :].reshape(rows, recv_ref.shape[2]).T
    save = pltpu.make_async_copy(enct_ref, enct_out, moved.at[0, layers])
    save.start()
    saves.append(save)
    for layer in reversed(range(layers)):
        loads[layer].wait()
        for x in range(local):
            actt_ref[layer, x] = act_ref[layer, x].T
        saves[layer].start()
    for save in saves:
        save.wait()


def render_kernel(
    local,
    capacity,
    me_ref,
    raws_ref,
    rank_ref,
    name_ref,
    laid_ref,
    act_ref,
    rendered_out,
    gslot_ref,
    headpart_ref,
    wide,
    dense,
    grad,
    ranked_ref,
    rendered_ref,
    moved,
):
    save = pltpu.make_async_copy(rendered_ref, rendered_out, moved)
    sources, samples = rank_ref.shape
    owners, pairs = raws_ref.shape[0], raws_ref.shape[1] // sources
    channels = pairs // local
    me = me_ref[0]
    wide[...] = raws_ref[...].astype(F32)
    chunks = samples // LANES
    member = iota((pairs, samples), 0) // channels

    def unslot(s, carry):
        name = name_ref[pl.ds(s, 1), :]
        at = pl.ds(pl.multiple_of(s * pairs, pairs), pairs)
        block = wide[:, at, :].reshape(owners * pairs, capacity).astype(BF16)
        pick = hot(iota((capacity, samples), 0) == rank_ref[pl.ds(s, 1), :])
        ranked_ref[s] = pick
        spread = dot(block, pick)
        total = jnp.zeros((pairs, samples), F32)
        for o in range(owners):
            total = total + jnp.where(name - o * local == member, spread[o * pairs : (o + 1) * pairs], 0.0)
        flat = total[:channels]
        for x in range(1, local):
            flat = flat + total[x * channels : (x + 1) * channels]
        for k in range(chunks):
            for c in range(channels):
                dense[c, pl.ds(s * chunks + k, 1), :] = flat[c : c + 1, k * LANES : (k + 1) * LANES]
        return carry

    lax.fori_loop(0, sources, unslot, 0, unroll=4)

    shades, graw = composite(
        [dense[c] for c in range(channels)],
        laid_ref[0],
        [laid_ref[c] for c in range(1, channels)],
        [laid_ref[c] for c in range(channels, 2 * channels - 1)],
    )
    for c in range(channels):
        grad[c] = graw[c]
    rays = samples // RAY_SAMPLES
    per_row = LANES // RAY_SAMPLES
    pick = hot(iota((LANES, rays), 0) == iota((LANES, rays), 1) % per_row * RAY_SAMPLES, F32)
    keep = iota((chunks, rays), 1) // per_row == iota((chunks, rays), 0)
    for c in range(channels - 1):
        dense[c] = shades[c]
        mine = dense[c, pl.ds(pl.multiple_of(me * chunks, chunks), chunks), :]
        mine = jnp.dot(mine, pick, precision=lax.Precision.HIGHEST, preferred_element_type=F32)
        rendered_ref[c : c + 1, :] = jnp.sum(jnp.where(keep, mine, 0.0), axis=0, keepdims=True)
    save.start()

    parts = [[] for _ in range(local)]
    for s in range(sources):
        own = name_ref[s : s + 1, :] - me * local == member
        flat = jnp.concatenate([lane_row(grad[c, s * chunks : (s + 1) * chunks, :]) for c in range(channels)], axis=0)
        high, low = split(jnp.where(own, jnp.concatenate([flat] * local, axis=0), 0.0))
        got = dot_nt(jnp.concatenate([high, low], axis=0), ranked_ref[s])
        for x in range(local):
            parts[x].append(
                jnp.concatenate(
                    [got[x * channels : (x + 1) * channels], got[pairs + x * channels : pairs + (x + 1) * channels]],
                    axis=0,
                )
            )
    head_total = None
    for x in range(local):
        part = jnp.concatenate(parts[x], axis=1).astype(BF16)
        gslot_ref[x] = part
        add = dot(part, act_ref[x])
        head_total = add if head_total is None else head_total + add
    head_total = head_total[:channels] + head_total[channels:]
    for d in range(headpart_ref.shape[0]):
        headpart_ref[d] = head_total
    save.wait()


def backward_kernel(copies, me_ref, slope_in, actt_in, enct_in, hidden_in, gslot_ref, head_ref, *rest):
    outs, (gfirst, ghidden, slope_ref, actt_ref, enct_ref, hidden_ref, moved) = rest[: 2 * copies], rest[2 * copies :]
    local = gslot_ref.shape[0]
    layers = hidden_ref.shape[1] + 1
    fetch = [(slope_in.at[layers - 1], slope_ref.at[layers - 1]), (hidden_in, hidden_ref)]
    for layer in reversed(range(layers - 1)):
        fetch.append((slope_in.at[layer], slope_ref.at[layer]))
        fetch.append((actt_in.at[layer], actt_ref.at[layer]))
    fetch.append((enct_in, enct_ref))
    loads = [pltpu.make_async_copy(a, b, moved.at[i]) for i, (a, b) in enumerate(fetch)]
    for load in loads:
        load.start()
    head = head_ref[...] * 0.5
    head = jnp.concatenate([head, head], axis=0)
    up = [dot_tn(gslot_ref[x], head).astype(BF16) for x in range(local)]
    loads.pop(0).wait()
    glin = [up[x] * slope_ref[layers - 1, x] for x in range(local)]
    loads.pop(0).wait()
    for layer in reversed(range(1, layers)):
        up = [dot_nt(glin[x], hidden_ref[x, layer - 1] * 0.5).astype(BF16) for x in range(local)]
        loads.pop(0).wait()
        loads.pop(0).wait()
        for x in range(local):
            ghidden[x, layer - 1] = dot(actt_ref[layer - 1, x], glin[x])
            glin[x] = up[x] * slope_ref[layer - 1, x]
    loads.pop(0).wait()
    for x in range(local):
        gfirst[x] = dot(enct_ref[x], glin[x])
    me = me_ref[0]
    for s in range(copies):
        first_out, hidden_out = outs[2 * s], outs[2 * s + 1]
        piece = lax.rem(me + s, copies)
        size = first_out.shape[1]
        first_out[...] = gfirst[:, pl.ds(pl.multiple_of(piece * size, size), size), :]
        size = hidden_out.shape[2]
        hidden_out[...] = ghidden[:, :, pl.ds(pl.multiple_of(piece * size, size), size), :]


def head_kernel(heads_ref, out_ref):
    out_ref[...] = jnp.sum(heads_ref[...], axis=0)


def sum_kernel(copies, head_ref, *refs):
    pieces, outs, (first_ref, hidden_ref, done) = refs[: 2 * copies], refs[2 * copies : 2 * copies + 3], refs[2 * copies + 3 :]
    pltpu.make_async_copy(head_ref, outs[2], done.at[2]).start()
    for k, held in enumerate((hidden_ref, first_ref)):
        total = pieces[1 - k][...]
        for s in range(1, copies):
            total = total + pieces[2 * s + 1 - k][...]
        held[...] = total
        pltpu.make_async_copy(held, outs[1 - k], done.at[k]).start()
    for k, held in enumerate((hidden_ref, first_ref)):
        pltpu.make_async_copy(held, outs[1 - k], done.at[k]).wait()
    pltpu.make_async_copy(head_ref, outs[2], done.at[2]).wait()


def shape(dims, dtype):
    return jax.ShapeDtypeStruct(dims, dtype)


def call(kernel, outs, ins, scratch=(), scalars=0, outside=(0, 0), flops=0, limit=24):
    specs = [pl.BlockSpec(memory_space=pltpu.SMEM)] * scalars
    specs += [pl.BlockSpec(memory_space=pl.ANY)] * outside[0]
    specs += [pl.BlockSpec(memory_space=VMEM)] * (len(ins) - len(specs))
    out_specs = [pl.BlockSpec(memory_space=pl.ANY)] * outside[1]
    out_specs += [pl.BlockSpec(memory_space=VMEM)] * (len(outs) - len(out_specs))
    held = [
        x if i < scalars else pltpu.with_memory_space_constraint(x, pltpu.HBM if i < scalars + outside[0] else VMEM)
        for i, x in enumerate(ins)
    ]
    return pl.pallas_call(
        kernel,
        out_shape=[
            (pltpu.HBM if i < outside[1] else VMEM)(x.shape, x.dtype) for i, x in enumerate(outs)
        ],
        in_specs=specs,
        out_specs=out_specs,
        scratch_shapes=list(scratch),
        cost_estimate=pl.CostEstimate(flops=flops, bytes_accessed=0, transcendentals=0),
        compiler_params=pltpu.CompilerParams(vmem_limit_bytes=limit * 1024 * 1024),
    )(*held)


def per_device(
    encoded, region_id, spacing, frame_index, target_rgb, frame_code, first_weight, hidden_weight, head_weight
):
    owners, copies = lax.axis_size("expert"), lax.axis_size("replica")
    local = first_weight.shape[0]
    experts = owners * local
    samples, enc_width = encoded.shape
    capacity = 2 * samples // experts
    hid = first_weight.shape[2]
    layers = hidden_weight.shape[1] + 1
    channels = head_weight.shape[0]
    chunks = samples // LANES
    slots = local * capacity
    rows = owners * capacity
    owner = lax.axis_index("expert").astype(jnp.int32).reshape(1)
    copy = lax.axis_index("replica").astype(jnp.int32).reshape(1)

    inputs = [
        region_id.reshape(chunks, LANES),
        encoded,
        spacing.reshape(chunks, LANES),
        frame_index.reshape(1, -1),
        target_rgb,
        frame_code,
    ]
    (outbound,) = call(
        functools.partial(dispatch_kernel, experts, capacity),
        [shape((owners, slots + META, enc_width), BF16)],
        inputs,
        [pltpu.VMEM(x.shape, x.dtype) for x in inputs]
        + [
            pltpu.VMEM((owners, slots + META, enc_width), BF16),
            pltpu.SemaphoreType.DMA((len(inputs),)),
            pltpu.SemaphoreType.DMA((owners,)),
        ],
        outside=(len(inputs), 1),
    )
    first_half, hidden_half, head = call(
        weight_kernel,
        [shape(first_weight.shape, BF16), shape(hidden_weight.shape, BF16), shape(head_weight.shape, BF16)],
        [first_weight, hidden_weight, head_weight],
        [
            pltpu.VMEM(first_weight.shape, BF16),
            pltpu.VMEM(hidden_weight.shape, BF16),
            pltpu.SemaphoreType.DMA((3,)),
        ],
        outside=(3, 0),
        flops=3 * 10**9,
    )
    recv = lax.all_to_all(outbound, "expert", split_axis=0, concat_axis=0, tiled=True)
    pairs = local * channels
    tile = 4
    top = (local, rows, hid)
    lower = (layers - 1,) + top
    acts, slopes, raw, act_top = call(
        functools.partial(forward_kernel, capacity, tile),
        [
            shape(lower, BF16),
            shape((layers,) + top, BF16),
            shape((owners, owners * pairs, capacity), BF16),
            shape(top, BF16),
        ],
        [recv, first_half, hidden_half, head],
        [
            pltpu.VMEM((owners * pairs, capacity), F32),
            pltpu.VMEM(lower, BF16),
            pltpu.VMEM((layers,) + top, BF16),
            pltpu.SemaphoreType.DMA((2, layers, owners // tile)),
        ],
        outside=(0, 2),
        flops=10**9,
    )
    raws = lax.all_to_all(raw, "expert", split_axis=0, concat_axis=0, tiled=True)
    flipped = (layers - 1, local, hid, rows)
    actt, enct, order, names, laid = call(
        functools.partial(plan_kernel, local, capacity),
        [
            shape(flipped, BF16),
            shape((local, enc_width, rows), BF16),
            shape((owners, samples), jnp.int32),
            shape((owners, samples), jnp.int32),
            shape((2 * channels - 1, owners * chunks, LANES), F32),
        ],
        [acts, recv],
        [
            pltpu.VMEM(lower, BF16),
            pltpu.VMEM(flipped, BF16),
            pltpu.VMEM((local, enc_width, rows), BF16),
            pltpu.SemaphoreType.DMA((2, layers)),
        ],
        outside=(1, 2),
        flops=5 * 10**9,
    )
    rendered, gslot, headpart = call(
        functools.partial(render_kernel, local, capacity),
        [
            shape(target_rgb.shape, F32),
            shape((local, 2 * channels, rows), BF16),
            shape((owners * copies, channels, hid), F32),
        ],
        [owner, raws, order, names, laid, act_top],
        [
            pltpu.VMEM((owners, owners * pairs, capacity), F32),
            pltpu.VMEM((channels, owners * chunks, LANES), F32),
            pltpu.VMEM((channels, owners * chunks, LANES), F32),
            pltpu.VMEM((owners, capacity, samples), BF16),
            pltpu.VMEM(target_rgb.shape, F32),
            pltpu.SemaphoreType.DMA,
        ],
        scalars=1,
        outside=(0, 1),
        flops=10**9,
    )
    heads = lax.all_to_all(headpart, ("expert", "replica"), split_axis=0, concat_axis=0, tiled=True)
    pieces = []
    for _ in range(copies):
        pieces.append(shape((local, enc_width // copies, hid), F32))
        pieces.append(shape((local, layers - 1, hid // copies, hid), F32))
    grads = call(
        functools.partial(backward_kernel, copies),
        pieces,
        [copy, slopes, actt, enct, hidden_weight, gslot, head],
        [
            pltpu.VMEM(first_weight.shape, F32),
            pltpu.VMEM(hidden_weight.shape, F32),
            pltpu.VMEM((layers,) + top, BF16),
            pltpu.VMEM(flipped, BF16),
            pltpu.VMEM((local, enc_width, rows), BF16),
            pltpu.VMEM(hidden_weight.shape, BF16),
            pltpu.SemaphoreType.DMA((2 * layers + 1,)),
        ],
        scalars=1,
        outside=(4, 0),
        flops=5 * 10**9,
    )
    grads = list(grads)
    for s in range(1, copies):
        ring = [(i, (i + s) % copies) for i in range(copies)]
        for k in (2 * s, 2 * s + 1):
            grads[k] = lax.ppermute(grads[k], "replica", ring)
    (head_grad,) = call(head_kernel, [shape((channels, hid), F32)], [heads], flops=10**11)
    first_grad, hidden_grad, head_grad = call(
        functools.partial(sum_kernel, copies),
        [shape(grads[0].shape, F32), shape(grads[1].shape, F32), shape((channels, hid), F32)],
        [head_grad, *grads],
        [pltpu.VMEM(grads[0].shape, F32), pltpu.VMEM(grads[1].shape, F32), pltpu.SemaphoreType.DMA((3,))],
        outside=(0, 3),
    )
    return (first_grad, hidden_grad, head_grad, rendered)


def solution(mesh):
    placed = (
        P(("groups", "expert", "replica"), None),
        P(("groups", "expert", "replica")),
        P(("groups", "expert", "replica")),
        P(("groups", "expert", "replica")),
        P(None, ("groups", "expert", "replica")),
        P(None, "groups"),
        P("expert", None, None),
        P("expert", None, None, None),
        P(),
    )
    return jax.shard_map(
        per_device,
        mesh=mesh,
        in_specs=placed,
        out_specs=(
            P(("groups", "expert"), "replica", None),
            P(("groups", "expert"), None, "replica", None),
            P("groups", None),
            P(None, ("groups", "expert", "replica")),
        ),
        check_vma=False,
    )
```

```python
import functools

import jax
import jax.numpy as jnp
from jax import lax
from jax.experimental import pallas as pl
from jax.experimental.pallas import tpu as pltpu
from jax.sharding import PartitionSpec as P

RAY_SAMPLES = 64
LANES = 128
META = 32
F32 = jnp.float32
BF16 = jnp.bfloat16
VMEM = pltpu.VMEM


def iota(shape, dim):
    return lax.broadcasted_iota(jnp.int32, shape, dim)


def hot(mask, dtype=BF16):
    return jnp.where(mask, 1.0, 0.0).astype(dtype)


def dot(a, b):
    return jnp.dot(a, b, preferred_element_type=F32)


def dot_nt(a, b):
    return lax.dot_general(a, b, (((1,), (1,)), ((), ())), preferred_element_type=F32)


def dot_tn(a, b):
    return lax.dot_general(a, b, (((0,), (0,)), ((), ())), preferred_element_type=F32)


def split(x):
    high = x.astype(BF16)
    return high, (x - high.astype(F32)).astype(BF16)


def lane_row(x):
    return jnp.concatenate([x[k : k + 1] for k in range(x.shape[0])], axis=1)


def ranks(region, experts):
    rows = region.shape[0]
    names = iota((experts, LANES), 0)
    upper = hot(iota((LANES, LANES), 0) <= iota((LANES, LANES), 1))
    equal = [hot(region[k : k + 1] == names, F32) for k in range(rows)]
    running = dot(jnp.concatenate(equal, axis=0).astype(BF16), upper)
    before = jnp.zeros((experts, 1), F32)
    out = []
    for k in range(rows):
        here = running[k * experts : (k + 1) * experts]
        out.append(jnp.sum(equal[k] * (here + before), axis=0, keepdims=True))
        before = before + here[:, LANES - 1 :]
    return jnp.concatenate(out, axis=0).astype(jnp.int32) - 1


def dispatch_kernel(experts, capacity, *refs):
    outside, out_ref, inside, (held, loaded, sent) = refs[:6], refs[6], refs[7:13], refs[13:]
    loads = [pltpu.make_async_copy(a, b, loaded.at[i]) for i, (a, b) in enumerate(zip(outside, inside))]
    for load in loads:
        load.start()
    region_ref, enc_ref, spacing_ref, frame_ref, target_ref, code_ref = inside
    owners, rows = held.shape[0], held.shape[1] - META
    samples = enc_ref.shape[0]
    loads[0].wait()
    region = region_ref[...]
    slot = lane_row(region * capacity + ranks(region, experts))
    for load in loads[1:]:
        load.wait()
    enc = enc_ref[...]

    frames = code_ref.shape[1]
    rays = frame_ref.shape[1]
    chosen = hot(frame_ref[...] == iota((frames, rays), 0), F32)
    bias = lax.dot_general(
        code_ref[...], chosen, (((1,), (0,)), ((), ())), precision=lax.Precision.HIGHEST, preferred_element_type=F32
    )
    small = jnp.concatenate([bias, target_ref[...], jnp.zeros((2, rays), F32)], axis=0)
    small_high, small_low = split(small)
    small = jnp.concatenate(
        [small_high.astype(F32), small_low.astype(F32), jnp.zeros((8, LANES - 2 * rays), F32)], axis=1
    )
    spacing_high, spacing_low = split(spacing_ref[...])
    meta = jnp.concatenate(
        [region.astype(F32), spacing_high.astype(F32), spacing_low.astype(F32), small], axis=0
    ).astype(BF16)

    def send(d):
        return pltpu.make_async_copy(held.at[d], out_ref.at[d], sent.at[d])

    def one(d, carry):
        pick = hot(iota((rows, samples), 0) == slot - d * rows)
        held[d, :rows, :] = dot(pick, enc).astype(BF16)
        held[d, rows:, :] = meta
        send(d).start()
        return carry

    lax.fori_loop(0, owners, one, 0, unroll=8)

    def finish(d, carry):
        send(d).wait()
        return carry

    lax.fori_loop(0, owners, finish, 0)


def weight_kernel(first_in, hidden_in, head_in, first_out, hidden_out, head_out, first_ref, hidden_ref, moved):
    loads = [
        pltpu.make_async_copy(first_in, first_ref, moved.at[0]),
        pltpu.make_async_copy(hidden_in, hidden_ref, moved.at[1]),
        pltpu.make_async_copy(head_in, head_out, moved.at[2]),
    ]
    for load in loads:
        load.start()
    for load in loads:
        load.wait()
    first_out[...] = first_ref[...] * 0.5
    hidden_out[...] = hidden_ref[...] * 0.5


def layer_forward(half):
    t = jnp.tanh(half)
    p = half * t
    return (half + p).astype(BF16), ((1.0 + t) * (1.0 + (half - p))).astype(BF16)


def forward_kernel(
    capacity,
    tile,
    recv_ref,
    first_ref,
    hidden_ref,
    head_ref,
    act_out,
    slope_out,
    raw_ref,
    held,
    act_ref,
    slope_ref,
    done,
):
    sources = recv_ref.shape[0]
    local = first_ref.shape[0]
    layers = hidden_ref.shape[1] + 1
    head = head_ref[...]
    pairs = local * head.shape[0]

    def rows_of(t):
        return pl.ds(pl.multiple_of(t * tile * capacity, tile * capacity), tile * capacity)

    def saves(t, layer):
        at = rows_of(t)
        pairs_of = [(slope_ref, slope_out), (act_ref, act_out)]
        return [
            pltpu.make_async_copy(a.at[layer, :, at, :], b.at[layer, :, at, :], done.at[k, layer, t])
            for k, (a, b) in enumerate(pairs_of)
        ]

    def step(t, carry):
        current = []
        for x in range(local):
            block = recv_ref[pl.ds(t * tile, tile), x * capacity : (x + 1) * capacity, :]
            current.append(block.reshape(tile * capacity, block.shape[2]))
        at = rows_of(t)
        for layer in range(layers):
            for x in range(local):
                weight = first_ref[x] if layer == 0 else hidden_ref[x, layer - 1]
                act, slope = layer_forward(dot(current[x], weight))
                slope_ref[layer, x, at, :] = slope
                act_ref[layer, x, at, :] = act
                current[x] = act
            for save in saves(t, layer):
                save.start()
        raws = [dot_nt(head, current[x]) for x in range(local)]
        for s in range(tile):
            both = jnp.concatenate([r[:, s * capacity : (s + 1) * capacity] for r in raws], axis=0)
            held[pl.ds(pl.multiple_of((t * tile + s) * pairs, pairs), pairs), :] = both
        return carry

    lax.fori_loop(0, sources // tile, step, 0)
    raw = held[...].astype(BF16)
    for d in range(raw_ref.shape[0]):
        raw_ref[d] = raw

    def finish(t, carry):
        for layer in range(layers):
            for save in saves(t, layer):
                save.wait()
        return carry

    lax.fori_loop(0, sources // tile, finish, 0)


def composite(raw, spacing, bias, target):
    row, col = iota((LANES, LANES), 0), iota((LANES, LANES), 1)
    same = row // RAY_SAMPLES == col // RAY_SAMPLES

    def along(x, mask):
        high, low = split(x)
        both = dot(jnp.concatenate([high, low], axis=1), jnp.concatenate([hot(mask)] * 2, axis=0))
        return both

    soft = jnp.maximum(raw[0], 0.0) + jnp.log1p(jnp.exp(-jnp.abs(raw[0])))
    optical = soft * spacing
    before = along(optical, same & (row < col))
    reach = jnp.exp(-before)
    left = jnp.exp(-optical)
    weight = reach * (1.0 - left)
    opacity = along(weight, same)
    rendered, graw = [], [None]
    pull = jnp.zeros_like(weight)
    for c in range(1, len(raw)):
        colour = jax.nn.sigmoid(raw[c] + bias[c - 1])
        shade = along(weight * colour, same) + (1.0 - opacity)
        off = shade - target[c - 1]
        rendered.append(shade)
        graw.append(off * weight * colour * (1.0 - colour))
        pull = pull + off * (colour - 1.0)
    optical_pull = pull * reach * left - along(pull * weight, same & (row > col))
    graw[0] = optical_pull * spacing * jax.nn.sigmoid(raw[0])
    return rendered, graw


def plan_kernel(
    local, capacity, act_in, recv_ref, actt_out, enct_out, ranked_ref, name_ref, laid_ref, act_ref, actt_ref, enct_ref, moved
):
    layers = actt_ref.shape[0]
    loads = [pltpu.make_async_copy(act_in.at[k], act_ref.at[k], moved.at[0, k]) for k in range(layers)]
    saves = [pltpu.make_async_copy(actt_ref.at[k], actt_out.at[k], moved.at[1, k]) for k in range(layers)]
    for load in loads:
        load.start()
    sources, slots = recv_ref.shape[0], recv_ref.shape[1] - META
    rows = sources * capacity
    experts = sources * local
    samples = ranked_ref.shape[2]
    chunks = samples // LANES

    def one(s, carry):
        region = recv_ref[s, slots : slots + chunks, :].astype(F32).astype(jnp.int32)
        ranked_ref[s] = hot(iota((capacity, samples), 0) == lane_row(ranks(region, experts)))
        name_ref[pl.ds(s, 1), :] = lane_row(region)
        return carry

    lax.fori_loop(0, sources, one, 0, unroll=2)

    rays = samples // RAY_SAMPLES
    per_row = rays // chunks
    meta = recv_ref[:, slots:, :].astype(F32)
    laid_ref[0] = (meta[:, chunks : 2 * chunks] + meta[:, 2 * chunks : 3 * chunks]).reshape(sources * chunks, LANES)
    small = meta[:, 3 * chunks :]
    lane = iota((chunks, LANES), 1)
    belongs = (lane % rays // per_row == iota((chunks, LANES), 0)) & (lane < 2 * rays)
    lay = hot(iota((LANES, LANES), 0) % per_row == iota((LANES, LANES), 1) // RAY_SAMPLES)
    for c in range(laid_ref.shape[0] - 1):
        parts = [jnp.where(belongs, small[s, c : c + 1, :], 0.0) for s in range(sources)]
        laid_ref[1 + c] = dot(jnp.concatenate(parts, axis=0).astype(BF16), lay)

    for x in range(local):
        enct_ref[x] = recv_ref[:, x * capacity : (x + 1) * capacity, :].reshape(rows, recv_ref.shape[2]).T
    save = pltpu.make_async_copy(enct_ref, enct_out, moved.at[0, layers])
    save.start()
    saves.append(save)
    for layer in reversed(range(layers)):
        loads[layer].wait()
        for x in range(local):
            actt_ref[layer, x] = act_ref[layer, x].T
        saves[layer].start()
    for save in saves:
        save.wait()


def render_kernel(
    local,
    capacity,
    me_ref,
    act_in,
    raws_ref,
    ranked_ref,
    name_ref,
    laid_ref,
    rendered_out,
    gslot_ref,
    headpart_ref,
    wide,
    dense,
    grad,
    act_ref,
    rendered_ref,
    moved,
):
    load = pltpu.make_async_copy(act_in.at[act_in.shape[0] - 1], act_ref, moved.at[0])
    save = pltpu.make_async_copy(rendered_ref, rendered_out, moved.at[1])
    load.start()
    sources, samples = ranked_ref.shape[0], ranked_ref.shape[2]
    owners, pairs = raws_ref.shape[0], raws_ref.shape[1] // sources
    channels = pairs // local
    me = me_ref[0]
    wide[...] = raws_ref[...].astype(F32)
    chunks = samples // LANES
    member = iota((pairs, samples), 0) // channels

    def unslot(s, carry):
        name = name_ref[pl.ds(s, 1), :]
        at = pl.ds(pl.multiple_of(s * pairs, pairs), pairs)
        block = wide[:, at, :].reshape(owners * pairs, capacity).astype(BF16)
        spread = dot(block, ranked_ref[s])
        total = jnp.zeros((pairs, samples), F32)
        for o in range(owners):
            total = total + jnp.where(name - o * local == member, spread[o * pairs : (o + 1) * pairs], 0.0)
        flat = total[:channels]
        for x in range(1, local):
            flat = flat + total[x * channels : (x + 1) * channels]
        for k in range(chunks):
            for c in range(channels):
                dense[c, pl.ds(s * chunks + k, 1), :] = flat[c : c + 1, k * LANES : (k + 1) * LANES]
        return carry

    lax.fori_loop(0, sources, unslot, 0, unroll=4)

    shades, graw = composite(
        [dense[c] for c in range(channels)],
        laid_ref[0],
        [laid_ref[c] for c in range(1, channels)],
        [laid_ref[c] for c in range(channels, 2 * channels - 1)],
    )
    for c in range(channels):
        grad[c] = graw[c]
    rays = samples // RAY_SAMPLES
    per_row = LANES // RAY_SAMPLES
    pick = hot(iota((LANES, rays), 0) == iota((LANES, rays), 1) % per_row * RAY_SAMPLES, F32)
    keep = iota((chunks, rays), 1) // per_row == iota((chunks, rays), 0)
    for c in range(channels - 1):
        dense[c] = shades[c]
        mine = dense[c, pl.ds(pl.multiple_of(me * chunks, chunks), chunks), :]
        mine = jnp.dot(mine, pick, precision=lax.Precision.HIGHEST, preferred_element_type=F32)
        rendered_ref[c : c + 1, :] = jnp.sum(jnp.where(keep, mine, 0.0), axis=0, keepdims=True)
    save.start()

    parts = [[] for _ in range(local)]
    for s in range(sources):
        own = name_ref[s : s + 1, :] - me * local == member
        flat = jnp.concatenate([lane_row(grad[c, s * chunks : (s + 1) * chunks, :]) for c in range(channels)], axis=0)
        high, low = split(jnp.where(own, jnp.concatenate([flat] * local, axis=0), 0.0))
        got = dot_nt(jnp.concatenate([high, low], axis=0), ranked_ref[s])
        for x in range(local):
            parts[x].append(
                jnp.concatenate(
                    [got[x * channels : (x + 1) * channels], got[pairs + x * channels : pairs + (x + 1) * channels]],
                    axis=0,
                )
            )
    load.wait()
    head_total = None
    for x in range(local):
        part = jnp.concatenate(parts[x], axis=1).astype(BF16)
        gslot_ref[x] = part
        add = dot(part, act_ref[x])
        head_total = add if head_total is None else head_total + add
    head_total = head_total[:channels] + head_total[channels:]
    for d in range(headpart_ref.shape[0]):
        headpart_ref[d] = head_total
    save.wait()


def backward_kernel(copies, me_ref, slope_in, actt_in, enct_in, hidden_in, gslot_ref, head_ref, *rest):
    outs, (gfirst, ghidden, slope_ref, actt_ref, enct_ref, hidden_ref, moved) = rest[: 2 * copies], rest[2 * copies :]
    local = gslot_ref.shape[0]
    layers = hidden_ref.shape[1] + 1
    fetch = [(slope_in.at[layers - 1], slope_ref.at[layers - 1]), (hidden_in, hidden_ref)]
    for layer in reversed(range(layers - 1)):
        fetch.append((slope_in.at[layer], slope_ref.at[layer]))
        fetch.append((actt_in.at[layer], actt_ref.at[layer]))
    fetch.append((enct_in, enct_ref))
    loads = [pltpu.make_async_copy(a, b, moved.at[i]) for i, (a, b) in enumerate(fetch)]
    for load in loads:
        load.start()
    head = head_ref[...] * 0.5
    head = jnp.concatenate([head, head], axis=0)
    up = [dot_tn(gslot_ref[x], head).astype(BF16) for x in range(local)]
    loads.pop(0).wait()
    glin = [up[x] * slope_ref[layers - 1, x] for x in range(local)]
    loads.pop(0).wait()
    for layer in reversed(range(1, layers)):
        up = [dot_nt(glin[x], hidden_ref[x, layer - 1] * 0.5).astype(BF16) for x in range(local)]
        loads.pop(0).wait()
        loads.pop(0).wait()
        for x in range(local):
            ghidden[x, layer - 1] = dot(actt_ref[layer - 1, x], glin[x])
            glin[x] = up[x] * slope_ref[layer - 1, x]
    loads.pop(0).wait()
    for x in range(local):
        gfirst[x] = dot(enct_ref[x], glin[x])
    me = me_ref[0]
    for s in range(copies):
        first_out, hidden_out = outs[2 * s], outs[2 * s + 1]
        piece = lax.rem(me + s, copies)
        size = first_out.shape[1]
        first_out[...] = gfirst[:, pl.ds(pl.multiple_of(piece * size, size), size), :]
        size = hidden_out.shape[2]
        hidden_out[...] = ghidden[:, :, pl.ds(pl.multiple_of(piece * size, size), size), :]


def head_kernel(heads_ref, out_ref):
    out_ref[...] = jnp.sum(heads_ref[...], axis=0)


def sum_kernel(copies, head_ref, *refs):
    pieces, outs, (first_ref, hidden_ref, done) = refs[: 2 * copies], refs[2 * copies : 2 * copies + 3], refs[2 * copies + 3 :]
    pltpu.make_async_copy(head_ref, outs[2], done.at[2]).start()
    for k, held in enumerate((hidden_ref, first_ref)):
        total = pieces[1 - k][...]
        for s in range(1, copies):
            total = total + pieces[2 * s + 1 - k][...]
        held[...] = total
        pltpu.make_async_copy(held, outs[1 - k], done.at[k]).start()
    for k, held in enumerate((hidden_ref, first_ref)):
        pltpu.make_async_copy(held, outs[1 - k], done.at[k]).wait()
    pltpu.make_async_copy(head_ref, outs[2], done.at[2]).wait()


def shape(dims, dtype):
    return jax.ShapeDtypeStruct(dims, dtype)


def call(kernel, outs, ins, scratch=(), scalars=0, outside=(0, 0), flops=0, limit=24):
    specs = [pl.BlockSpec(memory_space=pltpu.SMEM)] * scalars
    specs += [pl.BlockSpec(memory_space=pl.ANY)] * outside[0]
    specs += [pl.BlockSpec(memory_space=VMEM)] * (len(ins) - len(specs))
    out_specs = [pl.BlockSpec(memory_space=pl.ANY)] * outside[1]
    out_specs += [pl.BlockSpec(memory_space=VMEM)] * (len(outs) - len(out_specs))
    held = [
        x if i < scalars else pltpu.with_memory_space_constraint(x, pltpu.HBM if i < scalars + outside[0] else VMEM)
        for i, x in enumerate(ins)
    ]
    return pl.pallas_call(
        kernel,
        out_shape=[
            (pltpu.HBM if i < outside[1] else VMEM)(x.shape, x.dtype) for i, x in enumerate(outs)
        ],
        in_specs=specs,
        out_specs=out_specs,
        scratch_shapes=list(scratch),
        cost_estimate=pl.CostEstimate(flops=flops, bytes_accessed=0, transcendentals=0),
        compiler_params=pltpu.CompilerParams(vmem_limit_bytes=limit * 1024 * 1024),
    )(*held)


def per_device(
    encoded, region_id, spacing, frame_index, target_rgb, frame_code, first_weight, hidden_weight, head_weight
):
    owners, copies = lax.axis_size("expert"), lax.axis_size("replica")
    local = first_weight.shape[0]
    experts = owners * local
    samples, enc_width = encoded.shape
    capacity = 2 * samples // experts
    hid = first_weight.shape[2]
    layers = hidden_weight.shape[1] + 1
    channels = head_weight.shape[0]
    chunks = samples // LANES
    slots = local * capacity
    rows = owners * capacity
    owner = lax.axis_index("expert").astype(jnp.int32).reshape(1)
    copy = lax.axis_index("replica").astype(jnp.int32).reshape(1)

    inputs = [
        region_id.reshape(chunks, LANES),
        encoded,
        spacing.reshape(chunks, LANES),
        frame_index.reshape(1, -1),
        target_rgb,
        frame_code,
    ]
    (outbound,) = call(
        functools.partial(dispatch_kernel, experts, capacity),
        [shape((owners, slots + META, enc_width), BF16)],
        inputs,
        [pltpu.VMEM(x.shape, x.dtype) for x in inputs]
        + [
            pltpu.VMEM((owners, slots + META, enc_width), BF16),
            pltpu.SemaphoreType.DMA((len(inputs),)),
            pltpu.SemaphoreType.DMA((owners,)),
        ],
        outside=(len(inputs), 1),
    )
    first_half, hidden_half, head = call(
        weight_kernel,
        [shape(first_weight.shape, BF16), shape(hidden_weight.shape, BF16), shape(head_weight.shape, BF16)],
        [first_weight, hidden_weight, head_weight],
        [
            pltpu.VMEM(first_weight.shape, BF16),
            pltpu.VMEM(hidden_weight.shape, BF16),
            pltpu.SemaphoreType.DMA((3,)),
        ],
        outside=(3, 0),
        flops=3 * 10**9,
    )
    recv = lax.all_to_all(outbound, "expert", split_axis=0, concat_axis=0, tiled=True)
    pairs = local * channels
    tile = 4
    top = (local, rows, hid)
    lower = (layers - 1,) + top
    acts, slopes, raw = call(
        functools.partial(forward_kernel, capacity, tile),
        [
            shape((layers,) + top, BF16),
            shape((layers,) + top, BF16),
            shape((owners, owners * pairs, capacity), BF16),
        ],
        [recv, first_half, hidden_half, head],
        [
            pltpu.VMEM((owners * pairs, capacity), F32),
            pltpu.VMEM((layers,) + top, BF16),
            pltpu.VMEM((layers,) + top, BF16),
            pltpu.SemaphoreType.DMA((2, layers, owners // tile)),
        ],
        outside=(0, 2),
        flops=10**9,
    )
    raws = lax.all_to_all(raw, "expert", split_axis=0, concat_axis=0, tiled=True)
    flipped = (layers - 1, local, hid, rows)
    actt, enct, ranked, names, laid = call(
        functools.partial(plan_kernel, local, capacity),
        [
            shape(flipped, BF16),
            shape((local, enc_width, rows), BF16),
            shape((owners, capacity, samples), BF16),
            shape((owners, samples), jnp.int32),
            shape((2 * channels - 1, owners * chunks, LANES), F32),
        ],
        [acts, recv],
        [
            pltpu.VMEM(lower, BF16),
            pltpu.VMEM(flipped, BF16),
            pltpu.VMEM((local, enc_width, rows), BF16),
            pltpu.SemaphoreType.DMA((2, layers)),
        ],
        outside=(1, 2),
        flops=5 * 10**9,
    )
    rendered, gslot, headpart = call(
        functools.partial(render_kernel, local, capacity),
        [
            shape(target_rgb.shape, F32),
            shape((local, 2 * channels, rows), BF16),
            shape((owners * copies, channels, hid), F32),
        ],
        [owner, acts, raws, ranked, names, laid],
        [
            pltpu.VMEM((owners, owners * pairs, capacity), F32),
            pltpu.VMEM((channels, owners * chunks, LANES), F32),
            pltpu.VMEM((channels, owners * chunks, LANES), F32),
            pltpu.VMEM(top, BF16),
            pltpu.VMEM(target_rgb.shape, F32),
            pltpu.SemaphoreType.DMA((2,)),
        ],
        scalars=1,
        outside=(1, 1),
        flops=10**9,
    )
    heads = lax.all_to_all(headpart, ("expert", "replica"), split_axis=0, concat_axis=0, tiled=True)
    pieces = []
    for _ in range(copies):
        pieces.append(shape((local, enc_width // copies, hid), F32))
        pieces.append(shape((local, layers - 1, hid // copies, hid), F32))
    grads = call(
        functools.partial(backward_kernel, copies),
        pieces,
        [copy, slopes, actt, enct, hidden_weight, gslot, head],
        [
            pltpu.VMEM(first_weight.shape, F32),
            pltpu.VMEM(hidden_weight.shape, F32),
            pltpu.VMEM((layers,) + top, BF16),
            pltpu.VMEM(flipped, BF16),
            pltpu.VMEM((local, enc_width, rows), BF16),
            pltpu.VMEM(hidden_weight.shape, BF16),
            pltpu.SemaphoreType.DMA((2 * layers + 1,)),
        ],
        scalars=1,
        outside=(4, 0),
        flops=5 * 10**9,
    )
    grads = list(grads)
    for s in range(1, copies):
        ring = [(i, (i + s) % copies) for i in range(copies)]
        for k in (2 * s, 2 * s + 1):
            grads[k] = lax.ppermute(grads[k], "replica", ring)
    (head_grad,) = call(head_kernel, [shape((channels, hid), F32)], [heads], flops=10**11)
    first_grad, hidden_grad, head_grad = call(
        functools.partial(sum_kernel, copies),
        [shape(grads[0].shape, F32), shape(grads[1].shape, F32), shape((channels, hid), F32)],
        [head_grad, *grads],
        [pltpu.VMEM(grads[0].shape, F32), pltpu.VMEM(grads[1].shape, F32), pltpu.SemaphoreType.DMA((3,))],
        outside=(0, 3),
    )
    return (first_grad, hidden_grad, head_grad, rendered)


def solution(mesh):
    placed = (
        P(("groups", "expert", "replica"), None),
        P(("groups", "expert", "replica")),
        P(("groups", "expert", "replica")),
        P(("groups", "expert", "replica")),
        P(None, ("groups", "expert", "replica")),
        P(None, "groups"),
        P("expert", None, None),
        P("expert", None, None, None),
        P(),
    )
    return jax.shard_map(
        per_device,
        mesh=mesh,
        in_specs=placed,
        out_specs=(
            P(("groups", "expert"), "replica", None),
            P(("groups", "expert"), None, "replica", None),
            P("groups", None),
            P(None, ("groups", "expert", "replica")),
        ),
        check_vma=False,
    )
```

```python
import functools

import jax
import jax.numpy as jnp
from jax import lax
from jax.experimental import pallas as pl
from jax.experimental.pallas import tpu as pltpu
from jax.sharding import PartitionSpec as P

RAY_SAMPLES = 64
LANES = 128
META = 32
F32 = jnp.float32
BF16 = jnp.bfloat16
VMEM = pltpu.VMEM


def iota(shape, dim):
    return lax.broadcasted_iota(jnp.int32, shape, dim)


def hot(mask, dtype=BF16):
    return jnp.where(mask, 1.0, 0.0).astype(dtype)


def dot(a, b):
    return jnp.dot(a, b, preferred_element_type=F32)


def dot_nt(a, b):
    return lax.dot_general(a, b, (((1,), (1,)), ((), ())), preferred_element_type=F32)


def dot_tn(a, b):
    return lax.dot_general(a, b, (((0,), (0,)), ((), ())), preferred_element_type=F32)


def split(x):
    high = x.astype(BF16)
    return high, (x - high.astype(F32)).astype(BF16)


def lane_row(x):
    return jnp.concatenate([x[k : k + 1] for k in range(x.shape[0])], axis=1)


def ranks(region, experts):
    rows = region.shape[0]
    names = iota((experts, LANES), 0)
    upper = hot(iota((LANES, LANES), 0) <= iota((LANES, LANES), 1))
    equal = [hot(region[k : k + 1] == names, F32) for k in range(rows)]
    running = dot(jnp.concatenate(equal, axis=0).astype(BF16), upper)
    before = jnp.zeros((experts, 1), F32)
    out = []
    for k in range(rows):
        here = running[k * experts : (k + 1) * experts]
        out.append(jnp.sum(equal[k] * (here + before), axis=0, keepdims=True))
        before = before + here[:, LANES - 1 :]
    return jnp.concatenate(out, axis=0).astype(jnp.int32) - 1


def dispatch_kernel(experts, capacity, *refs):
    outside, out_ref, inside, (held, loaded, sent) = refs[:6], refs[6], refs[7:13], refs[13:]
    loads = [pltpu.make_async_copy(a, b, loaded.at[i]) for i, (a, b) in enumerate(zip(outside, inside))]
    for load in loads:
        load.start()
    region_ref, enc_ref, spacing_ref, frame_ref, target_ref, code_ref = inside
    owners, rows = held.shape[0], held.shape[1] - META
    samples = enc_ref.shape[0]
    loads[0].wait()
    region = region_ref[...]
    slot = lane_row(region * capacity + ranks(region, experts))
    for load in loads[1:]:
        load.wait()
    enc = enc_ref[...]

    frames = code_ref.shape[1]
    rays = frame_ref.shape[1]
    chosen = hot(frame_ref[...] == iota((frames, rays), 0), F32)
    bias = lax.dot_general(
        code_ref[...], chosen, (((1,), (0,)), ((), ())), precision=lax.Precision.HIGHEST, preferred_element_type=F32
    )
    small = jnp.concatenate([bias, target_ref[...], jnp.zeros((2, rays), F32)], axis=0)
    small_high, small_low = split(small)
    small = jnp.concatenate(
        [small_high.astype(F32), small_low.astype(F32), jnp.zeros((8, LANES - 2 * rays), F32)], axis=1
    )
    spacing_high, spacing_low = split(spacing_ref[...])
    meta = jnp.concatenate(
        [region.astype(F32), spacing_high.astype(F32), spacing_low.astype(F32), small], axis=0
    ).astype(BF16)

    def send(d):
        return pltpu.make_async_copy(held.at[d], out_ref.at[d], sent.at[d])

    def one(d, carry):
        pick = hot(iota((rows, samples), 0) == slot - d * rows)
        held[d, :rows, :] = dot(pick, enc).astype(BF16)
        held[d, rows:, :] = meta
        send(d).start()
        return carry

    lax.fori_loop(0, owners, one, 0, unroll=8)

    def finish(d, carry):
        send(d).wait()
        return carry

    lax.fori_loop(0, owners, finish, 0)


def weight_kernel(first_in, hidden_in, head_in, first_out, hidden_out, head_out, first_ref, hidden_ref, moved):
    loads = [
        pltpu.make_async_copy(first_in, first_ref, moved.at[0]),
        pltpu.make_async_copy(hidden_in, hidden_ref, moved.at[1]),
        pltpu.make_async_copy(head_in, head_out, moved.at[2]),
    ]
    for load in loads:
        load.start()
    for load in loads:
        load.wait()
    first_out[...] = first_ref[...] * 0.5
    hidden_out[...] = hidden_ref[...] * 0.5


def layer_forward(half):
    t = jnp.tanh(half)
    p = half * t
    return (half + p).astype(BF16), ((1.0 + t) * (1.0 + (half - p))).astype(BF16)


def forward_kernel(
    capacity,
    tile,
    recv_ref,
    first_ref,
    hidden_ref,
    head_ref,
    act_out,
    slope_out,
    raw_ref,
    held,
    act_ref,
    slope_ref,
    done,
):
    sources = recv_ref.shape[0]
    local = first_ref.shape[0]
    layers = hidden_ref.shape[1] + 1
    head = head_ref[...]
    pairs = local * head.shape[0]

    def rows_of(t):
        return pl.ds(pl.multiple_of(t * tile * capacity, tile * capacity), tile * capacity)

    def saves(t, layer):
        at = rows_of(t)
        pairs_of = [(slope_ref, slope_out), (act_ref, act_out)]
        return [
            pltpu.make_async_copy(a.at[layer, :, at, :], b.at[layer, :, at, :], done.at[k, layer, t])
            for k, (a, b) in enumerate(pairs_of)
        ]

    def step(t, carry):
        current = []
        for x in range(local):
            block = recv_ref[pl.ds(t * tile, tile), x * capacity : (x + 1) * capacity, :]
            current.append(block.reshape(tile * capacity, block.shape[2]))
        at = rows_of(t)
        for layer in range(layers):
            for x in range(local):
                weight = first_ref[x] if layer == 0 else hidden_ref[x, layer - 1]
                act, slope = layer_forward(dot(current[x], weight))
                slope_ref[layer, x, at, :] = slope
                act_ref[layer, x, at, :] = act
                current[x] = act
            for save in saves(t, layer):
                save.start()
        raws = [dot_nt(head, current[x]) for x in range(local)]
        for s in range(tile):
            both = jnp.concatenate([r[:, s * capacity : (s + 1) * capacity] for r in raws], axis=0)
            held[pl.ds(pl.multiple_of((t * tile + s) * pairs, pairs), pairs), :] = both
        return carry

    lax.fori_loop(0, sources // tile, step, 0)
    raw = held[...].astype(BF16)
    for d in range(raw_ref.shape[0]):
        raw_ref[d] = raw

    def finish(t, carry):
        for layer in range(layers):
            for save in saves(t, layer):
                save.wait()
        return carry

    lax.fori_loop(0, sources // tile, finish, 0)


def composite(raw, spacing, bias, target):
    row, col = iota((LANES, LANES), 0), iota((LANES, LANES), 1)
    same = row // RAY_SAMPLES == col // RAY_SAMPLES

    def along(x, mask):
        high, low = split(x)
        both = dot(jnp.concatenate([high, low], axis=1), jnp.concatenate([hot(mask)] * 2, axis=0))
        return both

    soft = jnp.maximum(raw[0], 0.0) + jnp.log1p(jnp.exp(-jnp.abs(raw[0])))
    optical = soft * spacing
    before = along(optical, same & (row < col))
    reach = jnp.exp(-before)
    left = jnp.exp(-optical)
    weight = reach * (1.0 - left)
    opacity = along(weight, same)
    rendered, graw = [], [None]
    pull = jnp.zeros_like(weight)
    for c in range(1, len(raw)):
        colour = jax.nn.sigmoid(raw[c] + bias[c - 1])
        shade = along(weight * colour, same) + (1.0 - opacity)
        off = shade - target[c - 1]
        rendered.append(shade)
        graw.append(off * weight * colour * (1.0 - colour))
        pull = pull + off * (colour - 1.0)
    optical_pull = pull * reach * left - along(pull * weight, same & (row > col))
    graw[0] = optical_pull * spacing * jax.nn.sigmoid(raw[0])
    return rendered, graw


def plan_kernel(
    local, capacity, act_in, recv_ref, actt_out, enct_out, ranked_ref, name_ref, laid_ref, act_ref, actt_ref, enct_ref, moved
):
    layers = actt_ref.shape[0]
    loads = [pltpu.make_async_copy(act_in.at[k], act_ref.at[k], moved.at[0, k]) for k in range(layers)]
    saves = [pltpu.make_async_copy(actt_ref.at[k], actt_out.at[k], moved.at[1, k]) for k in range(layers)]
    for load in loads:
        load.start()
    sources, slots = recv_ref.shape[0], recv_ref.shape[1] - META
    rows = sources * capacity
    experts = sources * local
    samples = ranked_ref.shape[2]
    chunks = samples // LANES

    def one(s, carry):
        region = recv_ref[s, slots:, :].astype(F32)[:chunks].astype(jnp.int32)
        ranked_ref[s] = hot(iota((capacity, samples), 0) == lane_row(ranks(region, experts)))
        name_ref[pl.ds(s, 1), :] = lane_row(region)
        return carry

    lax.fori_loop(0, sources, one, 0, unroll=2)

    rays = samples // RAY_SAMPLES
    per_row = rays // chunks
    meta = recv_ref[:, slots:, :].astype(F32)
    laid_ref[0] = (meta[:, chunks : 2 * chunks] + meta[:, 2 * chunks : 3 * chunks]).reshape(sources * chunks, LANES)
    small = meta[:, 3 * chunks :]
    lane = iota((chunks, LANES), 1)
    belongs = (lane % rays // per_row == iota((chunks, LANES), 0)) & (lane < 2 * rays)
    lay = hot(iota((LANES, LANES), 0) % per_row == iota((LANES, LANES), 1) // RAY_SAMPLES)
    for c in range(laid_ref.shape[0] - 1):
        parts = [jnp.where(belongs, small[s, c : c + 1, :], 0.0) for s in range(sources)]
        laid_ref[1 + c] = dot(jnp.concatenate(parts, axis=0).astype(BF16), lay)

    for x in range(local):
        enct_ref[x] = recv_ref[:, x * capacity : (x + 1) * capacity, :].reshape(rows, recv_ref.shape[2]).T
    save = pltpu.make_async_copy(enct_ref, enct_out, moved.at[0, layers])
    save.start()
    saves.append(save)
    for layer in reversed(range(layers)):
        loads[layer].wait()
        for x in range(local):
            actt_ref[layer, x] = act_ref[layer, x].T
        saves[layer].start()
    for save in saves:
        save.wait()


def render_kernel(
    local,
    capacity,
    me_ref,
    act_in,
    raws_ref,
    ranked_ref,
    name_ref,
    laid_ref,
    rendered_out,
    gslot_ref,
    headpart_ref,
    wide,
    dense,
    grad,
    act_ref,
    rendered_ref,
    moved,
):
    load = pltpu.make_async_copy(act_in.at[act_in.shape[0] - 1], act_ref, moved.at[0])
    save = pltpu.make_async_copy(rendered_ref, rendered_out, moved.at[1])
    load.start()
    sources, samples = ranked_ref.shape[0], ranked_ref.shape[2]
    owners, pairs = raws_ref.shape[0], raws_ref.shape[1] // sources
    channels = pairs // local
    me = me_ref[0]
    wide[...] = raws_ref[...].astype(F32)
    chunks = samples // LANES
    member = iota((pairs, samples), 0) // channels

    def unslot(s, carry):
        name = name_ref[pl.ds(s, 1), :]
        at = pl.ds(pl.multiple_of(s * pairs, pairs), pairs)
        block = wide[:, at, :].reshape(owners * pairs, capacity).astype(BF16)
        spread = dot(block, ranked_ref[s])
        total = jnp.zeros((pairs, samples), F32)
        for o in range(owners):
            total = total + jnp.where(name - o * local == member, spread[o * pairs : (o + 1) * pairs], 0.0)
        flat = total[:channels]
        for x in range(1, local):
            flat = flat + total[x * channels : (x + 1) * channels]
        for k in range(chunks):
            for c in range(channels):
                dense[c, pl.ds(s * chunks + k, 1), :] = flat[c : c + 1, k * LANES : (k + 1) * LANES]
        return carry

    lax.fori_loop(0, sources, unslot, 0, unroll=4)

    shades, graw = composite(
        [dense[c] for c in range(channels)],
        laid_ref[0],
        [laid_ref[c] for c in range(1, channels)],
        [laid_ref[c] for c in range(channels, 2 * channels - 1)],
    )
    for c in range(channels):
        grad[c] = graw[c]
    rays = samples // RAY_SAMPLES
    per_row = LANES // RAY_SAMPLES
    pick = hot(iota((LANES, rays), 0) == iota((LANES, rays), 1) % per_row * RAY_SAMPLES, F32)
    keep = iota((chunks, rays), 1) // per_row == iota((chunks, rays), 0)
    for c in range(channels - 1):
        dense[c] = shades[c]
        mine = dense[c, pl.ds(pl.multiple_of(me * chunks, chunks), chunks), :]
        mine = jnp.dot(mine, pick, precision=lax.Precision.HIGHEST, preferred_element_type=F32)
        rendered_ref[c : c + 1, :] = jnp.sum(jnp.where(keep, mine, 0.0), axis=0, keepdims=True)
    save.start()

    parts = [[] for _ in range(local)]
    for s in range(sources):
        own = name_ref[s : s + 1, :] - me * local == member
        flat = jnp.concatenate([lane_row(grad[c, s * chunks : (s + 1) * chunks, :]) for c in range(channels)], axis=0)
        high, low = split(jnp.where(own, jnp.concatenate([flat] * local, axis=0), 0.0))
        got = dot_nt(jnp.concatenate([high, low], axis=0), ranked_ref[s])
        for x in range(local):
            parts[x].append(
                jnp.concatenate(
                    [got[x * channels : (x + 1) * channels], got[pairs + x * channels : pairs + (x + 1) * channels]],
                    axis=0,
                )
            )
    load.wait()
    head_total = None
    for x in range(local):
        part = jnp.concatenate(parts[x], axis=1).astype(BF16)
        gslot_ref[x] = part
        add = dot(part, act_ref[x])
        head_total = add if head_total is None else head_total + add
    head_total = head_total[:channels] + head_total[channels:]
    for d in range(headpart_ref.shape[0]):
        headpart_ref[d] = head_total
    save.wait()


def backward_kernel(copies, me_ref, slope_in, actt_in, enct_in, hidden_in, gslot_ref, head_ref, *rest):
    outs, (gfirst, ghidden, slope_ref, actt_ref, enct_ref, hidden_ref, moved) = rest[: 2 * copies], rest[2 * copies :]
    local = gslot_ref.shape[0]
    layers = hidden_ref.shape[1] + 1
    fetch = [(slope_in.at[layers - 1], slope_ref.at[layers - 1]), (hidden_in, hidden_ref)]
    for layer in reversed(range(layers - 1)):
        fetch.append((slope_in.at[layer], slope_ref.at[layer]))
        fetch.append((actt_in.at[layer], actt_ref.at[layer]))
    fetch.append((enct_in, enct_ref))
    loads = [pltpu.make_async_copy(a, b, moved.at[i]) for i, (a, b) in enumerate(fetch)]
    for load in loads:
        load.start()
    head = head_ref[...] * 0.5
    head = jnp.concatenate([head, head], axis=0)
    up = [dot_tn(gslot_ref[x], head).astype(BF16) for x in range(local)]
    loads.pop(0).wait()
    glin = [up[x] * slope_ref[layers - 1, x] for x in range(local)]
    loads.pop(0).wait()
    for layer in reversed(range(1, layers)):
        up = [dot_nt(glin[x], hidden_ref[x, layer - 1] * 0.5).astype(BF16) for x in range(local)]
        loads.pop(0).wait()
        loads.pop(0).wait()
        for x in range(local):
            ghidden[x, layer - 1] = dot(actt_ref[layer - 1, x], glin[x])
            glin[x] = up[x] * slope_ref[layer - 1, x]
    loads.pop(0).wait()
    for x in range(local):
        gfirst[x] = dot(enct_ref[x], glin[x])
    me = me_ref[0]
    for s in range(copies):
        first_out, hidden_out = outs[2 * s], outs[2 * s + 1]
        piece = lax.rem(me + s, copies)
        size = first_out.shape[1]
        first_out[...] = gfirst[:, pl.ds(pl.multiple_of(piece * size, size), size), :]
        size = hidden_out.shape[2]
        hidden_out[...] = ghidden[:, :, pl.ds(pl.multiple_of(piece * size, size), size), :]


def head_kernel(heads_ref, out_ref):
    out_ref[...] = jnp.sum(heads_ref[...], axis=0)


def sum_kernel(copies, head_ref, *refs):
    pieces, outs, (first_ref, hidden_ref, done) = refs[: 2 * copies], refs[2 * copies : 2 * copies + 3], refs[2 * copies + 3 :]
    pltpu.make_async_copy(head_ref, outs[2], done.at[2]).start()
    for k, held in enumerate((hidden_ref, first_ref)):
        total = pieces[1 - k][...]
        for s in range(1, copies):
            total = total + pieces[2 * s + 1 - k][...]
        held[...] = total
        pltpu.make_async_copy(held, outs[1 - k], done.at[k]).start()
    for k, held in enumerate((hidden_ref, first_ref)):
        pltpu.make_async_copy(held, outs[1 - k], done.at[k]).wait()
    pltpu.make_async_copy(head_ref, outs[2], done.at[2]).wait()


def shape(dims, dtype):
    return jax.ShapeDtypeStruct(dims, dtype)


def call(kernel, outs, ins, scratch=(), scalars=0, outside=(0, 0), flops=0, limit=24):
    specs = [pl.BlockSpec(memory_space=pltpu.SMEM)] * scalars
    specs += [pl.BlockSpec(memory_space=pl.ANY)] * outside[0]
    specs += [pl.BlockSpec(memory_space=VMEM)] * (len(ins) - len(specs))
    out_specs = [pl.BlockSpec(memory_space=pl.ANY)] * outside[1]
    out_specs += [pl.BlockSpec(memory_space=VMEM)] * (len(outs) - len(out_specs))
    held = [
        x if i < scalars else pltpu.with_memory_space_constraint(x, pltpu.HBM if i < scalars + outside[0] else VMEM)
        for i, x in enumerate(ins)
    ]
    return pl.pallas_call(
        kernel,
        out_shape=[
            (pltpu.HBM if i < outside[1] else VMEM)(x.shape, x.dtype) for i, x in enumerate(outs)
        ],
        in_specs=specs,
        out_specs=out_specs,
        scratch_shapes=list(scratch),
        cost_estimate=pl.CostEstimate(flops=flops, bytes_accessed=0, transcendentals=0),
        compiler_params=pltpu.CompilerParams(vmem_limit_bytes=limit * 1024 * 1024),
    )(*held)


def per_device(
    encoded, region_id, spacing, frame_index, target_rgb, frame_code, first_weight, hidden_weight, head_weight
):
    owners, copies = lax.axis_size("expert"), lax.axis_size("replica")
    local = first_weight.shape[0]
    experts = owners * local
    samples, enc_width = encoded.shape
    capacity = 2 * samples // experts
    hid = first_weight.shape[2]
    layers = hidden_weight.shape[1] + 1
    channels = head_weight.shape[0]
    chunks = samples // LANES
    slots = local * capacity
    rows = owners * capacity
    owner = lax.axis_index("expert").astype(jnp.int32).reshape(1)
    copy = lax.axis_index("replica").astype(jnp.int32).reshape(1)

    inputs = [
        region_id.reshape(chunks, LANES),
        encoded,
        spacing.reshape(chunks, LANES),
        frame_index.reshape(1, -1),
        target_rgb,
        frame_code,
    ]
    (outbound,) = call(
        functools.partial(dispatch_kernel, experts, capacity),
        [shape((owners, slots + META, enc_width), BF16)],
        inputs,
        [pltpu.VMEM(x.shape, x.dtype) for x in inputs]
        + [
            pltpu.VMEM((owners, slots + META, enc_width), BF16),
            pltpu.SemaphoreType.DMA((len(inputs),)),
            pltpu.SemaphoreType.DMA((owners,)),
        ],
        outside=(len(inputs), 1),
    )
    first_half, hidden_half, head = call(
        weight_kernel,
        [shape(first_weight.shape, BF16), shape(hidden_weight.shape, BF16), shape(head_weight.shape, BF16)],
        [first_weight, hidden_weight, head_weight],
        [
            pltpu.VMEM(first_weight.shape, BF16),
            pltpu.VMEM(hidden_weight.shape, BF16),
            pltpu.SemaphoreType.DMA((3,)),
        ],
        outside=(3, 0),
        flops=3 * 10**9,
    )
    recv = lax.all_to_all(outbound, "expert", split_axis=0, concat_axis=0, tiled=True)
    pairs = local * channels
    tile = 4
    top = (local, rows, hid)
    lower = (layers - 1,) + top
    acts, slopes, raw = call(
        functools.partial(forward_kernel, capacity, tile),
        [
            shape((layers,) + top, BF16),
            shape((layers,) + top, BF16),
            shape((owners, owners * pairs, capacity), BF16),
        ],
        [recv, first_half, hidden_half, head],
        [
            pltpu.VMEM((owners * pairs, capacity), F32),
            pltpu.VMEM((layers,) + top, BF16),
            pltpu.VMEM((layers,) + top, BF16),
            pltpu.SemaphoreType.DMA((2, layers, owners // tile)),
        ],
        outside=(0, 2),
        flops=10**9,
    )
    raws = lax.all_to_all(raw, "expert", split_axis=0, concat_axis=0, tiled=True)
    flipped = (layers - 1, local, hid, rows)
    actt, enct, ranked, names, laid = call(
        functools.partial(plan_kernel, local, capacity),
        [
            shape(flipped, BF16),
            shape((local, enc_width, rows), BF16),
            shape((owners, capacity, samples), BF16),
            shape((owners, samples), jnp.int32),
            shape((2 * channels - 1, owners * chunks, LANES), F32),
        ],
        [acts, recv],
        [
            pltpu.VMEM(lower, BF16),
            pltpu.VMEM(flipped, BF16),
            pltpu.VMEM((local, enc_width, rows), BF16),
            pltpu.SemaphoreType.DMA((2, layers)),
        ],
        outside=(1, 2),
        flops=5 * 10**9,
    )
    rendered, gslot, headpart = call(
        functools.partial(render_kernel, local, capacity),
        [
            shape(target_rgb.shape, F32),
            shape((local, 2 * channels, rows), BF16),
            shape((owners * copies, channels, hid), F32),
        ],
        [owner, acts, raws, ranked, names, laid],
        [
            pltpu.VMEM((owners, owners * pairs, capacity), F32),
            pltpu.VMEM((channels, owners * chunks, LANES), F32),
            pltpu.VMEM((channels, owners * chunks, LANES), F32),
            pltpu.VMEM(top, BF16),
            pltpu.VMEM(target_rgb.shape, F32),
            pltpu.SemaphoreType.DMA((2,)),
        ],
        scalars=1,
        outside=(1, 1),
        flops=10**9,
    )
    heads = lax.all_to_all(headpart, ("expert", "replica"), split_axis=0, concat_axis=0, tiled=True)
    pieces = []
    for _ in range(copies):
        pieces.append(shape((local, enc_width // copies, hid), F32))
        pieces.append(shape((local, layers - 1, hid // copies, hid), F32))
    grads = call(
        functools.partial(backward_kernel, copies),
        pieces,
        [copy, slopes, actt, enct, hidden_weight, gslot, head],
        [
            pltpu.VMEM(first_weight.shape, F32),
            pltpu.VMEM(hidden_weight.shape, F32),
            pltpu.VMEM((layers,) + top, BF16),
            pltpu.VMEM(flipped, BF16),
            pltpu.VMEM((local, enc_width, rows), BF16),
            pltpu.VMEM(hidden_weight.shape, BF16),
            pltpu.SemaphoreType.DMA((2 * layers + 1,)),
        ],
        scalars=1,
        outside=(4, 0),
        flops=5 * 10**9,
    )
    grads = list(grads)
    for s in range(1, copies):
        ring = [(i, (i + s) % copies) for i in range(copies)]
        for k in (2 * s, 2 * s + 1):
            grads[k] = lax.ppermute(grads[k], "replica", ring)
    (head_grad,) = call(head_kernel, [shape((channels, hid), F32)], [heads], flops=10**11)
    first_grad, hidden_grad, head_grad = call(
        functools.partial(sum_kernel, copies),
        [shape(grads[0].shape, F32), shape(grads[1].shape, F32), shape((channels, hid), F32)],
        [head_grad, *grads],
        [pltpu.VMEM(grads[0].shape, F32), pltpu.VMEM(grads[1].shape, F32), pltpu.SemaphoreType.DMA((3,))],
        outside=(0, 3),
    )
    return (first_grad, hidden_grad, head_grad, rendered)


def solution(mesh):
    placed = (
        P(("groups", "expert", "replica"), None),
        P(("groups", "expert", "replica")),
        P(("groups", "expert", "replica")),
        P(("groups", "expert", "replica")),
        P(None, ("groups", "expert", "replica")),
        P(None, "groups"),
        P("expert", None, None),
        P("expert", None, None, None),
        P(),
    )
    return jax.shard_map(
        per_device,
        mesh=mesh,
        in_specs=placed,
        out_specs=(
            P(("groups", "expert"), "replica", None),
            P(("groups", "expert"), None, "replica", None),
            P("groups", None),
            P(None, ("groups", "expert", "replica")),
        ),
        check_vma=False,
    )
```

```python
import functools

import jax
import jax.numpy as jnp
from jax import lax
from jax.experimental import pallas as pl
from jax.experimental.pallas import tpu as pltpu
from jax.sharding import PartitionSpec as P

RAY_SAMPLES = 64
LANES = 128
META = 32
F32 = jnp.float32
BF16 = jnp.bfloat16
VMEM = pltpu.VMEM


def iota(shape, dim):
    return lax.broadcasted_iota(jnp.int32, shape, dim)


def hot(mask, dtype=BF16):
    return jnp.where(mask, 1.0, 0.0).astype(dtype)


def dot(a, b):
    return jnp.dot(a, b, preferred_element_type=F32)


def dot_nt(a, b):
    return lax.dot_general(a, b, (((1,), (1,)), ((), ())), preferred_element_type=F32)


def dot_tn(a, b):
    return lax.dot_general(a, b, (((0,), (0,)), ((), ())), preferred_element_type=F32)


def split(x):
    high = x.astype(BF16)
    return high, (x - high.astype(F32)).astype(BF16)


def lane_row(x):
    return jnp.concatenate([x[k : k + 1] for k in range(x.shape[0])], axis=1)


def ranks(region, experts):
    rows = region.shape[0]
    names = iota((experts, LANES), 0)
    upper = hot(iota((LANES, LANES), 0) <= iota((LANES, LANES), 1))
    equal = [hot(region[k : k + 1] == names, F32) for k in range(rows)]
    running = dot(jnp.concatenate(equal, axis=0).astype(BF16), upper)
    before = jnp.zeros((experts, 1), F32)
    out = []
    for k in range(rows):
        here = running[k * experts : (k + 1) * experts]
        out.append(jnp.sum(equal[k] * (here + before), axis=0, keepdims=True))
        before = before + here[:, LANES - 1 :]
    return jnp.concatenate(out, axis=0).astype(jnp.int32) - 1


def dispatch_kernel(experts, capacity, *refs):
    outside, out_ref, inside, (held, loaded, sent) = refs[:6], refs[6], refs[7:13], refs[13:]
    loads = [pltpu.make_async_copy(a, b, loaded.at[i]) for i, (a, b) in enumerate(zip(outside, inside))]
    for load in loads:
        load.start()
    region_ref, enc_ref, spacing_ref, frame_ref, target_ref, code_ref = inside
    owners, rows = held.shape[0], held.shape[1] - META
    samples = enc_ref.shape[0]
    loads[0].wait()
    region = region_ref[...]
    slot = lane_row(region * capacity + ranks(region, experts))
    for load in loads[1:]:
        load.wait()
    enc = enc_ref[...]

    frames = code_ref.shape[1]
    rays = frame_ref.shape[1]
    chosen = hot(frame_ref[...] == iota((frames, rays), 0), F32)
    bias = lax.dot_general(
        code_ref[...], chosen, (((1,), (0,)), ((), ())), precision=lax.Precision.HIGHEST, preferred_element_type=F32
    )
    small = jnp.concatenate([bias, target_ref[...], jnp.zeros((2, rays), F32)], axis=0)
    small_high, small_low = split(small)
    small = jnp.concatenate(
        [small_high.astype(F32), small_low.astype(F32), jnp.zeros((8, LANES - 2 * rays), F32)], axis=1
    )
    spacing_high, spacing_low = split(spacing_ref[...])
    meta = jnp.concatenate(
        [region.astype(F32), spacing_high.astype(F32), spacing_low.astype(F32), small], axis=0
    ).astype(BF16)

    def send(d):
        return pltpu.make_async_copy(held.at[d], out_ref.at[d], sent.at[d])

    def one(d, carry):
        pick = hot(iota((rows, samples), 0) == slot - d * rows)
        held[d, :rows, :] = dot(pick, enc).astype(BF16)
        held[d, rows:, :] = meta
        send(d).start()
        return carry

    lax.fori_loop(0, owners, one, 0, unroll=8)

    def finish(d, carry):
        send(d).wait()
        return carry

    lax.fori_loop(0, owners, finish, 0)


def weight_kernel(first_in, hidden_in, head_in, first_out, hidden_out, head_out, first_ref, hidden_ref, moved):
    loads = [
        pltpu.make_async_copy(first_in, first_ref, moved.at[0]),
        pltpu.make_async_copy(hidden_in, hidden_ref, moved.at[1]),
        pltpu.make_async_copy(head_in, head_out, moved.at[2]),
    ]
    for load in loads:
        load.start()
    for load in loads:
        load.wait()
    first_out[...] = first_ref[...] * 0.5
    hidden_out[...] = hidden_ref[...] * 0.5


def layer_forward(half):
    t = jnp.tanh(half)
    p = half * t
    return (half + p).astype(BF16), ((1.0 + t) * (1.0 + (half - p))).astype(BF16)


def forward_kernel(
    capacity,
    tile,
    recv_ref,
    first_ref,
    hidden_ref,
    head_ref,
    act_out,
    slope_out,
    raw_ref,
    held,
    act_ref,
    slope_ref,
    done,
):
    sources = recv_ref.shape[0]
    local = first_ref.shape[0]
    layers = hidden_ref.shape[1] + 1
    head = head_ref[...]
    pairs = local * head.shape[0]

    def rows_of(t):
        return pl.ds(pl.multiple_of(t * tile * capacity, tile * capacity), tile * capacity)

    def saves(t, layer):
        at = rows_of(t)
        pairs_of = [(slope_ref, slope_out), (act_ref, act_out)]
        return [
            pltpu.make_async_copy(a.at[layer, :, at, :], b.at[layer, :, at, :], done.at[k, layer, t])
            for k, (a, b) in enumerate(pairs_of)
        ]

    def step(t, carry):
        current = []
        for x in range(local):
            block = recv_ref[pl.ds(t * tile, tile), x * capacity : (x + 1) * capacity, :]
            current.append(block.reshape(tile * capacity, block.shape[2]))
        at = rows_of(t)
        for layer in range(layers):
            for x in range(local):
                weight = first_ref[x] if layer == 0 else hidden_ref[x, layer - 1]
                act, slope = layer_forward(dot(current[x], weight))
                slope_ref[layer, x, at, :] = slope
                act_ref[layer, x, at, :] = act
                current[x] = act
            for save in saves(t, layer):
                save.start()
        raws = [dot_nt(head, current[x]) for x in range(local)]
        for s in range(tile):
            both = jnp.concatenate([r[:, s * capacity : (s + 1) * capacity] for r in raws], axis=0)
            held[pl.ds(pl.multiple_of((t * tile + s) * pairs, pairs), pairs), :] = both
        return carry

    lax.fori_loop(0, sources // tile, step, 0)
    raw = held[...].astype(BF16)
    for d in range(raw_ref.shape[0]):
        raw_ref[d] = raw

    def finish(t, carry):
        for layer in range(layers):
            for save in saves(t, layer):
                save.wait()
        return carry

    lax.fori_loop(0, sources // tile, finish, 0)


def composite(raw, spacing, bias, target):
    row, col = iota((LANES, LANES), 0), iota((LANES, LANES), 1)
    same = row // RAY_SAMPLES == col // RAY_SAMPLES

    def along(x, mask):
        high, low = split(x)
        both = dot(jnp.concatenate([high, low], axis=1), jnp.concatenate([hot(mask)] * 2, axis=0))
        return both

    soft = jnp.maximum(raw[0], 0.0) + jnp.log1p(jnp.exp(-jnp.abs(raw[0])))
    optical = soft * spacing
    before = along(optical, same & (row < col))
    reach = jnp.exp(-before)
    left = jnp.exp(-optical)
    weight = reach * (1.0 - left)
    opacity = along(weight, same)
    rendered, graw = [], [None]
    pull = jnp.zeros_like(weight)
    for c in range(1, len(raw)):
        colour = jax.nn.sigmoid(raw[c] + bias[c - 1])
        shade = along(weight * colour, same) + (1.0 - opacity)
        off = shade - target[c - 1]
        rendered.append(shade)
        graw.append(off * weight * colour * (1.0 - colour))
        pull = pull + off * (colour - 1.0)
    optical_pull = pull * reach * left - along(pull * weight, same & (row > col))
    graw[0] = optical_pull * spacing * jax.nn.sigmoid(raw[0])
    return rendered, graw


def plan_kernel(
    local, capacity, act_in, recv_ref, actt_out, enct_out, ranked_ref, name_ref, laid_ref, act_ref, actt_ref, enct_ref, moved
):
    layers = actt_ref.shape[0]
    loads = [pltpu.make_async_copy(act_in.at[k], act_ref.at[k], moved.at[0, k]) for k in range(layers)]
    saves = [pltpu.make_async_copy(actt_ref.at[k], actt_out.at[k], moved.at[1, k]) for k in range(layers)]
    for load in loads:
        load.start()
    sources, slots = recv_ref.shape[0], recv_ref.shape[1] - META
    rows = sources * capacity
    experts = sources * local
    samples = ranked_ref.shape[2]
    chunks = samples // LANES

    def one(s, carry):
        region = recv_ref[s, slots:, :].astype(F32)[:chunks].astype(jnp.int32)
        ranked_ref[s] = hot(iota((capacity, samples), 0) == lane_row(ranks(region, experts)))
        name_ref[pl.ds(s, 1), :] = lane_row(region)
        return carry

    lax.fori_loop(0, sources, one, 0, unroll=2)

    rays = samples // RAY_SAMPLES
    per_row = rays // chunks
    meta = recv_ref[:, slots:, :].astype(F32)
    laid_ref[0] = (meta[:, chunks : 2 * chunks] + meta[:, 2 * chunks : 3 * chunks]).reshape(sources * chunks, LANES)
    small = meta[:, 3 * chunks :]
    lane = iota((chunks, LANES), 1)
    belongs = (lane % rays // per_row == iota((chunks, LANES), 0)) & (lane < 2 * rays)
    lay = hot(iota((LANES, LANES), 0) % per_row == iota((LANES, LANES), 1) // RAY_SAMPLES)
    for c in range(laid_ref.shape[0] - 1):
        parts = [jnp.where(belongs, small[s, c : c + 1, :], 0.0) for s in range(sources)]
        laid_ref[1 + c] = dot(jnp.concatenate(parts, axis=0).astype(BF16), lay)

    for x in range(local):
        enct_ref[x] = recv_ref[:, x * capacity : (x + 1) * capacity, :].reshape(rows, recv_ref.shape[2]).T
    save = pltpu.make_async_copy(enct_ref, enct_out, moved.at[0, layers])
    save.start()
    saves.append(save)
    for layer in reversed(range(layers)):
        loads[layer].wait()
        for x in range(local):
            actt_ref[layer, x] = act_ref[layer, x].T
        saves[layer].start()
    for save in saves:
        save.wait()


def render_kernel(
    local,
    capacity,
    me_ref,
    act_in,
    raws_ref,
    ranked_ref,
    name_ref,
    laid_ref,
    rendered_out,
    gslot_ref,
    headpart_ref,
    wide,
    dense,
    grad,
    act_ref,
    rendered_ref,
    moved,
):
    load = pltpu.make_async_copy(act_in.at[act_in.shape[0] - 1], act_ref, moved.at[0])
    save = pltpu.make_async_copy(rendered_ref, rendered_out, moved.at[1])
    load.start()
    sources, samples = ranked_ref.shape[0], ranked_ref.shape[2]
    owners, pairs = raws_ref.shape[0], raws_ref.shape[1] // sources
    channels = pairs // local
    me = me_ref[0]
    wide[...] = raws_ref[...].astype(F32)
    chunks = samples // LANES
    member = iota((pairs, samples), 0) // channels

    def unslot(s, carry):
        name = name_ref[pl.ds(s, 1), :]
        at = pl.ds(pl.multiple_of(s * pairs, pairs), pairs)
        block = wide[:, at, :].reshape(owners * pairs, capacity).astype(BF16)
        spread = dot(block, ranked_ref[s])
        total = jnp.zeros((pairs, samples), F32)
        for o in range(owners):
            total = total + jnp.where(name - o * local == member, spread[o * pairs : (o + 1) * pairs], 0.0)
        flat = total[:channels]
        for x in range(1, local):
            flat = flat + total[x * channels : (x + 1) * channels]
        rows = pl.ds(pl.multiple_of(s * chunks, chunks), chunks)
        for c in range(channels):
            pieces = [flat[c : c + 1, k * LANES : (k + 1) * LANES] for k in range(chunks)]
            dense[c, rows, :] = jnp.concatenate(pieces, axis=0)
        return carry

    lax.fori_loop(0, sources, unslot, 0, unroll=4)

    shades, graw = composite(
        [dense[c] for c in range(channels)],
        laid_ref[0],
        [laid_ref[c] for c in range(1, channels)],
        [laid_ref[c] for c in range(channels, 2 * channels - 1)],
    )
    for c in range(channels):
        grad[c] = graw[c]
    rays = samples // RAY_SAMPLES
    per_row = LANES // RAY_SAMPLES
    pick = hot(iota((LANES, rays), 0) == iota((LANES, rays), 1) % per_row * RAY_SAMPLES, F32)
    keep = iota((chunks, rays), 1) // per_row == iota((chunks, rays), 0)
    for c in range(channels - 1):
        dense[c] = shades[c]
        mine = dense[c, pl.ds(pl.multiple_of(me * chunks, chunks), chunks), :]
        mine = jnp.dot(mine, pick, precision=lax.Precision.HIGHEST, preferred_element_type=F32)
        rendered_ref[c : c + 1, :] = jnp.sum(jnp.where(keep, mine, 0.0), axis=0, keepdims=True)
    save.start()

    parts = [[] for _ in range(local)]
    for s in range(sources):
        own = name_ref[s : s + 1, :] - me * local == member
        flat = jnp.concatenate([lane_row(grad[c, s * chunks : (s + 1) * chunks, :]) for c in range(channels)], axis=0)
        high, low = split(jnp.where(own, jnp.concatenate([flat] * local, axis=0), 0.0))
        got = dot_nt(jnp.concatenate([high, low], axis=0), ranked_ref[s])
        for x in range(local):
            parts[x].append(
                jnp.concatenate(
                    [got[x * channels : (x + 1) * channels], got[pairs + x * channels : pairs + (x + 1) * channels]],
                    axis=0,
                )
            )
    load.wait()
    head_total = None
    for x in range(local):
        part = jnp.concatenate(parts[x], axis=1).astype(BF16)
        gslot_ref[x] = part
        add = dot(part, act_ref[x])
        head_total = add if head_total is None else head_total + add
    head_total = head_total[:channels] + head_total[channels:]
    for d in range(headpart_ref.shape[0]):
        headpart_ref[d] = head_total
    save.wait()


def backward_kernel(copies, me_ref, slope_in, actt_in, enct_in, hidden_in, gslot_ref, head_ref, *rest):
    outs, (gfirst, ghidden, slope_ref, actt_ref, enct_ref, hidden_ref, moved) = rest[: 2 * copies], rest[2 * copies :]
    local = gslot_ref.shape[0]
    layers = hidden_ref.shape[1] + 1
    fetch = [(slope_in.at[layers - 1], slope_ref.at[layers - 1]), (hidden_in, hidden_ref)]
    for layer in reversed(range(layers - 1)):
        fetch.append((slope_in.at[layer], slope_ref.at[layer]))
        fetch.append((actt_in.at[layer], actt_ref.at[layer]))
    fetch.append((enct_in, enct_ref))
    loads = [pltpu.make_async_copy(a, b, moved.at[i]) for i, (a, b) in enumerate(fetch)]
    for load in loads:
        load.start()
    head = head_ref[...] * 0.5
    head = jnp.concatenate([head, head], axis=0)
    up = [dot_tn(gslot_ref[x], head).astype(BF16) for x in range(local)]
    loads.pop(0).wait()
    glin = [up[x] * slope_ref[layers - 1, x] for x in range(local)]
    loads.pop(0).wait()
    for layer in reversed(range(1, layers)):
        up = [dot_nt(glin[x], hidden_ref[x, layer - 1] * 0.5).astype(BF16) for x in range(local)]
        loads.pop(0).wait()
        loads.pop(0).wait()
        for x in range(local):
            ghidden[x, layer - 1] = dot(actt_ref[layer - 1, x], glin[x])
            glin[x] = up[x] * slope_ref[layer - 1, x]
    loads.pop(0).wait()
    for x in range(local):
        gfirst[x] = dot(enct_ref[x], glin[x])
    me = me_ref[0]
    for s in range(copies):
        first_out, hidden_out = outs[2 * s], outs[2 * s + 1]
        piece = lax.rem(me + s, copies)
        size = first_out.shape[1]
        first_out[...] = gfirst[:, pl.ds(pl.multiple_of(piece * size, size), size), :]
        size = hidden_out.shape[2]
        hidden_out[...] = ghidden[:, :, pl.ds(pl.multiple_of(piece * size, size), size), :]


def head_kernel(heads_ref, out_ref):
    out_ref[...] = jnp.sum(heads_ref[...], axis=0)


def sum_kernel(copies, head_ref, *refs):
    pieces, outs, (first_ref, hidden_ref, done) = refs[: 2 * copies], refs[2 * copies : 2 * copies + 3], refs[2 * copies + 3 :]
    pltpu.make_async_copy(head_ref, outs[2], done.at[2]).start()
    for k, held in enumerate((hidden_ref, first_ref)):
        total = pieces[1 - k][...]
        for s in range(1, copies):
            total = total + pieces[2 * s + 1 - k][...]
        held[...] = total
        pltpu.make_async_copy(held, outs[1 - k], done.at[k]).start()
    for k, held in enumerate((hidden_ref, first_ref)):
        pltpu.make_async_copy(held, outs[1 - k], done.at[k]).wait()
    pltpu.make_async_copy(head_ref, outs[2], done.at[2]).wait()


def shape(dims, dtype):
    return jax.ShapeDtypeStruct(dims, dtype)


def call(kernel, outs, ins, scratch=(), scalars=0, outside=(0, 0), flops=0, limit=24):
    specs = [pl.BlockSpec(memory_space=pltpu.SMEM)] * scalars
    specs += [pl.BlockSpec(memory_space=pl.ANY)] * outside[0]
    specs += [pl.BlockSpec(memory_space=VMEM)] * (len(ins) - len(specs))
    out_specs = [pl.BlockSpec(memory_space=pl.ANY)] * outside[1]
    out_specs += [pl.BlockSpec(memory_space=VMEM)] * (len(outs) - len(out_specs))
    held = [
        x if i < scalars else pltpu.with_memory_space_constraint(x, pltpu.HBM if i < scalars + outside[0] else VMEM)
        for i, x in enumerate(ins)
    ]
    return pl.pallas_call(
        kernel,
        out_shape=[
            (pltpu.HBM if i < outside[1] else VMEM)(x.shape, x.dtype) for i, x in enumerate(outs)
        ],
        in_specs=specs,
        out_specs=out_specs,
        scratch_shapes=list(scratch),
        cost_estimate=pl.CostEstimate(flops=flops, bytes_accessed=0, transcendentals=0),
        compiler_params=pltpu.CompilerParams(vmem_limit_bytes=limit * 1024 * 1024),
    )(*held)


def per_device(
    encoded, region_id, spacing, frame_index, target_rgb, frame_code, first_weight, hidden_weight, head_weight
):
    owners, copies = lax.axis_size("expert"), lax.axis_size("replica")
    local = first_weight.shape[0]
    experts = owners * local
    samples, enc_width = encoded.shape
    capacity = 2 * samples // experts
    hid = first_weight.shape[2]
    layers = hidden_weight.shape[1] + 1
    channels = head_weight.shape[0]
    chunks = samples // LANES
    slots = local * capacity
    rows = owners * capacity
    owner = lax.axis_index("expert").astype(jnp.int32).reshape(1)
    copy = lax.axis_index("replica").astype(jnp.int32).reshape(1)

    inputs = [
        region_id.reshape(chunks, LANES),
        encoded,
        spacing.reshape(chunks, LANES),
        frame_index.reshape(1, -1),
        target_rgb,
        frame_code,
    ]
    (outbound,) = call(
        functools.partial(dispatch_kernel, experts, capacity),
        [shape((owners, slots + META, enc_width), BF16)],
        inputs,
        [pltpu.VMEM(x.shape, x.dtype) for x in inputs]
        + [
            pltpu.VMEM((owners, slots + META, enc_width), BF16),
            pltpu.SemaphoreType.DMA((len(inputs),)),
            pltpu.SemaphoreType.DMA((owners,)),
        ],
        outside=(len(inputs), 1),
    )
    first_half, hidden_half, head = call(
        weight_kernel,
        [shape(first_weight.shape, BF16), shape(hidden_weight.shape, BF16), shape(head_weight.shape, BF16)],
        [first_weight, hidden_weight, head_weight],
        [
            pltpu.VMEM(first_weight.shape, BF16),
            pltpu.VMEM(hidden_weight.shape, BF16),
            pltpu.SemaphoreType.DMA((3,)),
        ],
        outside=(3, 0),
        flops=3 * 10**9,
    )
    recv = lax.all_to_all(outbound, "expert", split_axis=0, concat_axis=0, tiled=True)
    pairs = local * channels
    tile = 4
    top = (local, rows, hid)
    lower = (layers - 1,) + top
    acts, slopes, raw = call(
        functools.partial(forward_kernel, capacity, tile),
        [
            shape((layers,) + top, BF16),
            shape((layers,) + top, BF16),
            shape((owners, owners * pairs, capacity), BF16),
        ],
        [recv, first_half, hidden_half, head],
        [
            pltpu.VMEM((owners * pairs, capacity), F32),
            pltpu.VMEM((layers,) + top, BF16),
            pltpu.VMEM((layers,) + top, BF16),
            pltpu.SemaphoreType.DMA((2, layers, owners // tile)),
        ],
        outside=(0, 2),
        flops=10**9,
    )
    raws = lax.all_to_all(raw, "expert", split_axis=0, concat_axis=0, tiled=True)
    flipped = (layers - 1, local, hid, rows)
    actt, enct, ranked, names, laid = call(
        functools.partial(plan_kernel, local, capacity),
        [
            shape(flipped, BF16),
            shape((local, enc_width, rows), BF16),
            shape((owners, capacity, samples), BF16),
            shape((owners, samples), jnp.int32),
            shape((2 * channels - 1, owners * chunks, LANES), F32),
        ],
        [acts, recv],
        [
            pltpu.VMEM(lower, BF16),
            pltpu.VMEM(flipped, BF16),
            pltpu.VMEM((local, enc_width, rows), BF16),
            pltpu.SemaphoreType.DMA((2, layers)),
        ],
        outside=(1, 2),
        flops=5 * 10**9,
    )
    rendered, gslot, headpart = call(
        functools.partial(render_kernel, local, capacity),
        [
            shape(target_rgb.shape, F32),
            shape((local, 2 * channels, rows), BF16),
            shape((owners * copies, channels, hid), F32),
        ],
        [owner, acts, raws, ranked, names, laid],
        [
            pltpu.VMEM((owners, owners * pairs, capacity), F32),
            pltpu.VMEM((channels, owners * chunks, LANES), F32),
            pltpu.VMEM((channels, owners * chunks, LANES), F32),
            pltpu.VMEM(top, BF16),
            pltpu.VMEM(target_rgb.shape, F32),
            pltpu.SemaphoreType.DMA((2,)),
        ],
        scalars=1,
        outside=(1, 1),
        flops=10**9,
    )
    heads = lax.all_to_all(headpart, ("expert", "replica"), split_axis=0, concat_axis=0, tiled=True)
    pieces = []
    for _ in range(copies):
        pieces.append(shape((local, enc_width // copies, hid), F32))
        pieces.append(shape((local, layers - 1, hid // copies, hid), F32))
    grads = call(
        functools.partial(backward_kernel, copies),
        pieces,
        [copy, slopes, actt, enct, hidden_weight, gslot, head],
        [
            pltpu.VMEM(first_weight.shape, F32),
            pltpu.VMEM(hidden_weight.shape, F32),
            pltpu.VMEM((layers,) + top, BF16),
            pltpu.VMEM(flipped, BF16),
            pltpu.VMEM((local, enc_width, rows), BF16),
            pltpu.VMEM(hidden_weight.shape, BF16),
            pltpu.SemaphoreType.DMA((2 * layers + 1,)),
        ],
        scalars=1,
        outside=(4, 0),
        flops=5 * 10**9,
    )
    grads = list(grads)
    for s in range(1, copies):
        ring = [(i, (i + s) % copies) for i in range(copies)]
        for k in (2 * s, 2 * s + 1):
            grads[k] = lax.ppermute(grads[k], "replica", ring)
    (head_grad,) = call(head_kernel, [shape((channels, hid), F32)], [heads], flops=10**11)
    first_grad, hidden_grad, head_grad = call(
        functools.partial(sum_kernel, copies),
        [shape(grads[0].shape, F32), shape(grads[1].shape, F32), shape((channels, hid), F32)],
        [head_grad, *grads],
        [pltpu.VMEM(grads[0].shape, F32), pltpu.VMEM(grads[1].shape, F32), pltpu.SemaphoreType.DMA((3,))],
        outside=(0, 3),
    )
    return (first_grad, hidden_grad, head_grad, rendered)


def solution(mesh):
    placed = (
        P(("groups", "expert", "replica"), None),
        P(("groups", "expert", "replica")),
        P(("groups", "expert", "replica")),
        P(("groups", "expert", "replica")),
        P(None, ("groups", "expert", "replica")),
        P(None, "groups"),
        P("expert", None, None),
        P("expert", None, None, None),
        P(),
    )
    return jax.shard_map(
        per_device,
        mesh=mesh,
        in_specs=placed,
        out_specs=(
            P(("groups", "expert"), "replica", None),
            P(("groups", "expert"), None, "replica", None),
            P("groups", None),
            P(None, ("groups", "expert", "replica")),
        ),
        check_vma=False,
    )
```
